256 devices in a mesh: ctx: 64 (over z_hi, x, y, core), tp: 4 (over z_lo).
Axes of the slice: x: 4, y: 4, z: 8 (z_hi: 2, z_lo: 4; z = z_hi * 4 + z_lo), core: 2. Of those that a mesh axis runs over, the one named last changes fastest.
Arguments:
- queries: bfloat16 [8192, 4096], P(('ctx', 'tp')), may hold values from -180 to 180
- keys: bfloat16 [8192, 512], P(('ctx', 'tp')), may hold values from -6 to 6
- values: bfloat16 [8192, 512], P(('ctx', 'tp')), may hold values from -6 to 6
- out_grad: bfloat16 [8192, 4096], P(('ctx', 'tp')), may hold values from -6 to 6
- doc_lengths: int32 [16], replicated, may hold values from 1 to 2048, 8192 in all
- row_block: int32 [128], replicated, may hold values from 0 to 127, as said below
Outputs:
- attended: bfloat16 [8192, 4096], P(('ctx', 'tp'))
- query_grad: bfloat16 [8192, 4096], P(('ctx', 'tp'))
- key_grad: bfloat16 [8192, 512], P(('ctx', 'tp'))
- value_grad: bfloat16 [8192, 512], P(('ctx', 'tp'))
The draws below stay inside these ranges and needn't reach their ends.
Inputs may be any that keep to these rules, and one draw needn't show every extreme that they name: `doc_lengths`: they add up to 8192; the longest is exactly 2048. `row_block`: each block number appears once; the two slots 2c and 2c + 1 of context shard c hold blocks k and 127 - k for some k.
All inputs are finite; a program needn't handle non-finite values.
Results may differ from the reference program's by a relative error of at most 0.039.
Values may be sent and summed in bfloat16 or wider, within the bound.
A program may use at most 64 MiB of HBM per device.

```python
import math
import jax
import jax.numpy as jnp
import numpy as np
from jax import lax

HEADS = 32
KV_HEADS = 4
HEAD = 128
DOCS = 16
GROUP = 8
QF = 4096
KF = 512
SEQ = 8192
NBLK = 128
LONGEST = 2048


def shared_keys(key):
    base = jax.random.normal(jax.random.fold_in(key, 101), (SEQ, KV_HEADS * HEAD), jnp.float32)
    return jnp.clip(base, -6.0, 6.0)


def draw_keys(key, part):
    return shared_keys(key).astype(jnp.bfloat16)


def draw_queries(key, part):
    own_key = jax.random.fold_in(key, 3)
    drawn = jnp.clip(jax.random.normal(own_key, (SEQ, HEADS * HEAD), jnp.float32), -6.0, 6.0)
    return drawn.astype(jnp.bfloat16)


def draw_row_block(key, part):
    key = jax.random.fold_in(key, 5)
    order = jax.random.permutation(jax.random.fold_in(key, 1), NBLK // 2).astype(jnp.int32)
    flip = jax.random.randint(jax.random.fold_in(key, 2), (NBLK // 2,), 0, 2)
    first = jnp.where(flip == 1, NBLK - 1 - order, order)
    second = NBLK - 1 - first
    return jnp.stack([first, second], axis=1).reshape(NBLK).astype(jnp.int32)


def shard_levels(rng, dims, shards, smallest, largest):
    loudness, own = 1.0, jax.random.fold_in(rng, 6)
    for axis_at, parts in shards:
        steps = jnp.exp(jax.random.uniform(jax.random.fold_in(own, axis_at), (parts,), jnp.float32, smallest / len(shards), largest / len(shards)))
        loudness = loudness * jnp.repeat(steps, dims[axis_at] // parts).reshape([-1 if axis == axis_at else 1 for axis in range(len(dims))])
    return loudness


def split_up(count, total, reach, slope):
    loads = [(1 << 20) // math.isqrt(standing ** slope) + 1 for standing in range(2, count + 1)]
    spare, holding = total - reach - (count - 1), [1] * (count - 1)
    while spare > 0:
        movable = [i for i in range(count - 1) if holding[i] < reach]
        pool, remaining = sum([loads[i] for i in movable]), spare
        for i in movable:
            more = min(reach - holding[i], max(1, remaining * loads[i] // pool), spare)
            holding[i] = holding[i] + more
            spare = spare - more
    return np.array([reach] + holding)


def ragged(key, count, total, reach, skew):
    if count == 2:
        one = jax.random.randint(key, (), max(1, total - reach), min(reach, total - 1) + 1)
        return jnp.stack([one, total - one])
    lengths = jnp.asarray(split_up(count, total, reach, skew), jnp.int32)
    twos = (count - 1) // 2
    donor, sink = lengths[1:1 + 2 * twos:2], lengths[2:2 + 2 * twos:2]
    margin = jnp.minimum(donor - 1, reach - sink)
    moved = jax.random.randint(jax.random.fold_in(key, 1), (twos,), 0, 1 << 20) % (margin + 1)
    lengths = lengths.at[1:1 + 2 * twos:2].set(donor - moved).at[2:2 + 2 * twos:2].set(sink + moved)
    return lengths[jax.random.permutation(jax.random.fold_in(key, 2), count)]


def normal_values(key, dims, deviation, bound, pieces=(), kind=jnp.bfloat16):
    values = jax.random.normal(key, dims, jnp.float32) * deviation
    if len(pieces) > 0:
        values = shard_levels(key, dims, pieces, -0.22, 0.18) * values
    return jnp.clip(values, min=-bound, max=bound).astype(kind)


def setup_inputs(seed: int = 0) -> dict:
    splits = jax.random.split(jax.random.key(seed), 7)
    return {
        "queries": draw_queries(jax.random.fold_in(splits[6], 71), 0),
        "keys": draw_keys(jax.random.fold_in(splits[6], 71), 0),
        "values": normal_values(splits[2], (SEQ, KF), 1.0, 6.0, ((0, 256),)),
        "out_grad": normal_values(splits[3], (SEQ, QF), 1.0, 6.0, ((0, 256),)),
        "doc_lengths": ragged(splits[4], DOCS, SEQ, LONGEST, 2).astype(jnp.int32),
        "row_block": draw_row_block(jax.random.fold_in(splits[6], 71), 0),
    }


negative = -1e+30

def reference(queries, keys, values, out_grad, doc_lengths, row_block):
    block_rows = SEQ // NBLK
    offsets = jnp.arange(block_rows, dtype=jnp.int32)
    positions = (row_block[:, None] * block_rows + offsets[None, :]).reshape(SEQ)
    ends = jnp.cumsum(doc_lengths)
    documents = lax.optimization_barrier(jnp.sum((positions[:, None] >= ends[None, :]).astype(jnp.int32), axis=1))
    mask = (positions[None, :] <= positions[:, None]) & (documents[None, :] == documents[:, None])
    scale = 1.0 / math.sqrt(HEAD)
    q_heads = queries.reshape(SEQ, HEADS, HEAD).transpose(1, 0, 2)
    g_heads = out_grad.reshape(SEQ, HEADS, HEAD).transpose(1, 0, 2)
    k_heads = keys.reshape(SEQ, KV_HEADS, HEAD).transpose(1, 0, 2)
    v_heads = values.reshape(SEQ, KV_HEADS, HEAD).transpose(1, 0, 2)
    kv_index = jnp.arange(HEADS, dtype=jnp.int32) // GROUP

    def one_head(item):
        q_h, g_h, index = item
        k_g = k_heads[index]
        v_g = v_heads[index]
        scores = jnp.dot(q_h, k_g.T, preferred_element_type=jnp.float32) * scale
        masked = jnp.where(mask, scores, negative)
        top = lax.optimization_barrier(jnp.max(masked, axis=1, keepdims=True))
        weights = jnp.where(mask, jnp.exp(masked - top), 0.0)
        total = lax.optimization_barrier(jnp.sum(weights, axis=1, keepdims=True))
        attended = (jnp.dot(weights.astype(jnp.bfloat16), v_g, preferred_element_type=jnp.float32) / total).astype(jnp.bfloat16)
        log_total = top + jnp.log(total)
        probs = jnp.where(mask, jnp.exp(scores - log_total), 0.0)
        delta = lax.optimization_barrier(jnp.sum(g_h.astype(jnp.float32) * attended.astype(jnp.float32), axis=1, keepdims=True))
        d_probs = jnp.dot(g_h, v_g.T, preferred_element_type=jnp.float32)
        d_scores = (probs * (d_probs - delta) * scale).astype(jnp.bfloat16)
        query_grad = jnp.dot(d_scores, k_g, preferred_element_type=jnp.float32).astype(jnp.bfloat16)
        key_part = jnp.dot(d_scores.T, q_h, preferred_element_type=jnp.float32)
        value_part = jnp.dot(probs.astype(jnp.bfloat16).T, g_h, preferred_element_type=jnp.float32)
        return (attended, query_grad, key_part, value_part)
    attended, query_grad, key_part, value_part = lax.map(one_head, (q_heads, g_heads, kv_index))
    attended = attended.transpose(1, 0, 2).reshape(SEQ, HEADS * HEAD)
    query_grad = query_grad.transpose(1, 0, 2).reshape(SEQ, HEADS * HEAD)
    key_grad = lax.optimization_barrier(jnp.sum(key_part.reshape(KV_HEADS, GROUP, SEQ, HEAD), axis=1))
    value_grad = lax.optimization_barrier(jnp.sum(value_part.reshape(KV_HEADS, GROUP, SEQ, HEAD), axis=1))
    key_grad = key_grad.transpose(1, 0, 2).reshape(SEQ, KV_HEADS * HEAD).astype(jnp.bfloat16)
    value_grad = value_grad.transpose(1, 0, 2).reshape(SEQ, KV_HEADS * HEAD).astype(jnp.bfloat16)
    return (attended, query_grad, key_grad, value_grad)
```

```python
import math

import jax
import jax.numpy as jnp
from jax import lax
from jax.experimental import pallas as pl
from jax.experimental.pallas import tpu as pltpu
from jax.sharding import PartitionSpec as P

HEAD = 128
BLOCK = 64
GROUP = 8
DOCS = 16
NBLK = 128
ZH, X, Y, CORE, TP = 2, 4, 4, 2, 4
ROWS = 2 * BLOCK
MINE = ROWS // TP
WIDE = GROUP * HEAD
TILE = 256
PER_TILE = TILE // BLOCK
TILES = 9
LANES = GROUP * BLOCK
SCALE = 1.0 / math.sqrt(HEAD)
SCALE2 = SCALE * math.log2(math.e)
NEGATIVE = -1e30
VMEM_LIMIT = 56 * 1024 * 1024
f32 = jnp.float32
bf16 = jnp.bfloat16


def place():
    c = lax.axis_index("ctx")
    t = lax.axis_index("tp")
    return c // 32, (c // 8) % 4, (c // 2) % 4, c % 2, t


def ctx_of(zh, x, y, core):
    return ((zh * X + x) * Y + y) * CORE + core


def enter(zh, x, y, core, t):
    barrier = pltpu.get_barrier_semaphore()
    me = ctx_of(zh, x, y, core)
    peers = [(me, (t + d) % TP) for d in range(1, TP)]
    peers += [(ctx_of(zh, (x + d) % X, y, core), t) for d in range(1, X)]
    peers += [(ctx_of(zh, x, (y + d) % Y, core), t) for d in range(1, Y)]
    peers += [(ctx_of(1 - zh, x, y, core), t), (ctx_of(zh, x, y, 1 - core), t)]
    for peer in peers:
        pl.semaphore_signal(barrier, inc=1, device_id=peer, device_id_type=pl.DeviceIdType.MESH)
    pl.semaphore_wait(barrier, len(peers))


def remote(src, dst, send, recv, peer):
    return pltpu.make_async_remote_copy(
        src_ref=src,
        dst_ref=dst,
        send_sem=send,
        recv_sem=recv,
        device_id=peer,
        device_id_type=pl.DeviceIdType.MESH,
    )


def columns(index, width):
    return pl.ds(pl.multiple_of(index * width, width), width)


def rows_of(index, count):
    return pl.ds(pl.multiple_of(index * count, count), count)


def gather_kernel(
    q, k, v, g, q_o, g_o, kv_o,
    own_sem, tp_send, tp_recv, wide_send, wide_recv, z_send, z_recv,
    one_send, one_recv, two_send, two_recv, core_send, core_recv,
):
    zh, x, y, core, t = place()
    me = ctx_of(zh, x, y, core)
    enter(zh, x, y, core, t)
    own = kv_o.at[zh, x, y, core]
    sends = []

    small = []
    for d in (2, 1, 3):
        peer = (t + d) % TP
        for i, ref in enumerate((k, v)):
            copy = remote(
                ref.at[:, columns(peer, HEAD)],
                own.at[i, rows_of(t, MINE), :],
                tp_send.at[d - 1, i],
                tp_recv.at[d - 1, i],
                (me, peer),
            )
            copy.start()
            small.append(copy)
    local = []
    for i, ref in enumerate((k, v)):
        copy = pltpu.make_async_copy(
            ref.at[:, columns(t, HEAD)], own.at[i, rows_of(t, MINE), :], own_sem.at[i]
        )
        copy.start()
        local.append(copy)
    for i, (ref, out) in enumerate(((q, q_o), (g, g_o))):
        copy = pltpu.make_async_copy(
            ref.at[:, columns(t, WIDE)], out.at[rows_of(t, MINE), :], own_sem.at[2 + i]
        )
        copy.start()
        local.append(copy)
    for copy in small:
        copy.wait_recv()
    sends += small
    local[0].wait()
    local[1].wait()

    across = remote(own, own, z_send, z_recv, (ctx_of(1 - zh, x, y, core), t))
    across.start()
    across.wait_recv()
    sends.append(across)

    sibling = (ctx_of(zh, x, y, 1 - core), t)

    def x_peer(d):
        return (ctx_of(zh, (x + d) % X, y, core), t)

    def y_peer(d):
        return (ctx_of(zh, x, (y + d) % Y, core), t)

    def chunk(i, dx, dy, which):
        return kv_o.at[:, (x + dx) % X, (y + dy) % Y, which, i]

    firsts = {}
    for d in (2, 1, 3):
        for i in range(2):
            here = chunk(i, 0, 0, core)
            copy = remote(
                here, here, one_send.at[i, d - 1], one_recv.at[i, d - 1],
                x_peer(d) if i == 0 else y_peer(d),
            )
            copy.start()
            firsts[i, d] = copy
            sends.append(copy)

    wide = []
    for i, (ref, out) in enumerate(((q, q_o), (g, g_o))):
        for d in (2, 1, 3):
            peer = (t + d) % TP
            copy = remote(
                ref.at[:, columns(peer, WIDE)],
                out.at[rows_of(t, MINE), :],
                wide_send.at[i, d - 1],
                wide_recv.at[i, d - 1],
                (me, peer),
            )
            copy.start()
            wide.append(copy)
            sends.append(copy)

    seconds = {}
    siblings = []

    def spread(i, d):
        dx, dy = (-d, 0) if i == 0 else (0, -d)
        here = chunk(i, dx, dy, core)
        for e in (2, 1, 3):
            copy = remote(
                here, here, two_send.at[i, d, e - 1], two_recv.at[i, d, e - 1],
                y_peer(e) if i == 0 else x_peer(e),
            )
            copy.start()
            seconds[i, d, e] = copy
            sends.append(copy)
        to_sibling(i, d, 0)

    def to_sibling(i, d, e):
        dx, dy = (-d, -e) if i == 0 else (-e, -d)
        here = chunk(i, dx, dy, core)
        copy = remote(here, here, core_send.at[i, d, e], core_recv.at[i, d, e], sibling)
        copy.start()
        siblings.append(copy)
        sends.append(copy)

    spread(0, 0)
    spread(1, 0)
    for d in (1, 3, 2):
        for i in range(2):
            firsts[i, d].wait_recv()
            spread(i, d)
    for d in (0, 1, 3, 2):
        for e in (1, 3, 2):
            for i in range(2):
                seconds[i, d, e].wait_recv()
                to_sibling(i, d, e)
    for copy in siblings:
        copy.wait_recv()
    for copy in wide:
        copy.wait_recv()
    local[2].wait()
    local[3].wait()
    for copy in sends:
        copy.wait_send()


def gather(queries, keys, values, out_grad):
    dma = pltpu.SemaphoreType.DMA
    return pl.pallas_call(
        gather_kernel,
        out_shape=(
            jax.ShapeDtypeStruct((ROWS, WIDE), bf16),
            jax.ShapeDtypeStruct((ROWS, WIDE), bf16),
            jax.ShapeDtypeStruct((ZH, X, Y, CORE, 2, ROWS, HEAD), bf16),
        ),
        in_specs=[pl.BlockSpec(memory_space=pl.ANY)] * 4,
        out_specs=[pl.BlockSpec(memory_space=pl.ANY)] * 3,
        scratch_shapes=[
            dma((4,)),
            dma((3, 2)), dma((3, 2)),
            dma((2, 3)), dma((2, 3)),
            dma, dma,
            dma((2, 3)), dma((2, 3)),
            dma((2, 4, 3)), dma((2, 4, 3)),
            dma((2, 4, 4)), dma((2, 4, 4)),
        ],
        compiler_params=pltpu.CompilerParams(collective_id=0, has_side_effects=True),
        name="gather",
    )(queries, keys, values, out_grad)


def mm(a, b, ca, cb):
    return lax.dot_general(a, b, (((ca,), (cb,)), ((), ())), preferred_element_type=f32)


def attend_kernel(
    doc, row_block, q_ref, g_ref, kv_ref, att_ref, dq_ref, grad_ref,
    slot_of, s_scr, w_scr, qb, gb, qs, gs,
):
    c = lax.axis_index("ctx")

    def clear(i, carry):
        grad_ref[i] = jnp.zeros(grad_ref.shape[1:], bf16)
        return carry

    lax.fori_loop(0, grad_ref.shape[0], clear, 0)

    def invert(i, carry):
        slot_of[row_block[i]] = i
        return carry

    lax.fori_loop(0, NBLK, invert, 0)
    offset = lax.broadcasted_iota(jnp.int32, (1, LANES), 1) % BLOCK

    for b in range(2):
        block = row_block[2 * c + b]
        first = block * BLOCK
        position = first + offset
        low = jnp.zeros((1, LANES), jnp.int32)
        low_first = jnp.int32(0)
        end = jnp.int32(0)
        for d in range(DOCS):
            end = end + doc[d]
            low = jnp.where(position >= end, end, low)
            low_first = jnp.where(first >= end, end, low_first)
        start = low_first // BLOCK
        tiles = (block - start + PER_TILE) // PER_TILE

        here = pl.ds(b * BLOCK, BLOCK)
        for h in range(GROUP):
            qb[pl.ds(h * BLOCK, BLOCK), :] = q_ref[here, pl.ds(h * HEAD, HEAD)]
            gb[pl.ds(h * BLOCK, BLOCK), :] = g_ref[here, pl.ds(h * HEAD, HEAD)]

        def slots(tile):
            return [
                slot_of[jnp.minimum(start + tile * PER_TILE + i, NBLK - 1)] for i in range(PER_TILE)
            ]

        def load(which, tile):
            return jnp.concatenate([kv_ref[2 * (s // 2) + which, s % 2] for s in slots(tile)], axis=0)

        def scores(tile, top):
            s = mm(load(0, tile), qb[...], 1, 1)
            at = (start + tile * PER_TILE) * BLOCK + lax.broadcasted_iota(
                jnp.int32, (TILE, LANES), 0
            )
            s = jnp.where((at >= low) & (at <= position), s, NEGATIVE)
            s_scr[tile] = s
            return jnp.maximum(top, jnp.max(s.reshape(TILE // 8, 8, LANES), axis=0))

        top8 = lax.fori_loop(0, tiles, scores, jnp.full((8, LANES), NEGATIVE, f32))
        top = jnp.max(top8, axis=0, keepdims=True)

        def weigh(tile, state):
            total8, acc = state
            w = jnp.exp2((s_scr[tile] - top) * SCALE2)
            total8 = total8 + jnp.sum(w.reshape(TILE // 8, 8, LANES), axis=0)
            w16 = w.astype(bf16)
            w_scr[tile] = w16
            return total8, acc + mm(load(1, tile), w16, 0, 0)

        total8, acc = lax.fori_loop(
            0, tiles, weigh, (jnp.zeros((8, LANES), f32), jnp.zeros((HEAD, LANES), f32))
        )
        inv = 1.0 / jnp.sum(total8, axis=0, keepdims=True)
        att_t = acc * inv
        g_t = gb[...].astype(f32).T
        delta = jnp.sum(g_t * att_t, axis=0, keepdims=True)
        att = att_t.T.astype(bf16)
        inv_rows = jnp.broadcast_to(inv, (HEAD, LANES)).T
        gs[...] = (gb[...].astype(f32) * inv_rows).astype(bf16)
        qs[...] = (qb[...].astype(f32) * (inv_rows * SCALE)).astype(bf16)
        for h in range(GROUP):
            att_ref[here, pl.ds(h * HEAD, HEAD)] = att[h * BLOCK : (h + 1) * BLOCK]

        def back(tile, dq_t):
            keys = load(0, tile)
            dp = mm(load(1, tile), gb[...], 1, 1)
            w16 = w_scr[tile]
            ds = (w16.astype(f32) * (dp - delta)).astype(bf16)
            dq_t = dq_t + mm(keys, ds, 0, 0)
            dk = mm(ds, qs[...], 1, 0)
            dv = mm(w16, gs[...], 1, 0)
            for i, s in enumerate(slots(tile)):
                part = slice(i * BLOCK, (i + 1) * BLOCK)
                for which, add in ((0, dk), (1, dv)):
                    old = grad_ref[2 * (s // 2) + which, s % 2]
                    grad_ref[2 * (s // 2) + which, s % 2] = (old.astype(f32) + add[part]).astype(bf16)
            return dq_t

        dq_t = lax.fori_loop(0, tiles, back, jnp.zeros((HEAD, LANES), f32))
        dq = (dq_t * (inv * SCALE)).T.astype(bf16)
        for h in range(GROUP):
            dq_ref[here, pl.ds(h * HEAD, HEAD)] = dq[h * BLOCK : (h + 1) * BLOCK]


def attend(doc_lengths, row_block, q, g, kv):
    vmem = pl.BlockSpec(memory_space=pltpu.VMEM)
    smem = pl.BlockSpec(memory_space=pltpu.SMEM)
    kv = kv.reshape(NBLK, 2, BLOCK, HEAD)
    return pl.pallas_call(
        attend_kernel,
        out_shape=(
            jax.ShapeDtypeStruct((ROWS, WIDE), bf16),
            jax.ShapeDtypeStruct((ROWS, WIDE), bf16),
            jax.ShapeDtypeStruct((NBLK, 2, BLOCK, HEAD), bf16),
        ),
        in_specs=[smem, smem, vmem, vmem, vmem],
        out_specs=[vmem] * 3,
        scratch_shapes=[
            pltpu.SMEM((NBLK,), jnp.int32),
            pltpu.VMEM((TILES, TILE, LANES), f32),
            pltpu.VMEM((TILES, TILE, LANES), bf16),
            pltpu.VMEM((LANES, HEAD), bf16),
            pltpu.VMEM((LANES, HEAD), bf16),
            pltpu.VMEM((LANES, HEAD), bf16),
            pltpu.VMEM((LANES, HEAD), bf16),
        ],
        compiler_params=pltpu.CompilerParams(vmem_limit_bytes=VMEM_LIMIT),
        name="attend",
    )(doc_lengths, row_block, q, g, kv)


def scatter_kernel(
    att, dq, grad, att_o, dq_o, dk_o, dv_o,
    in_core, held, in_one, held_two, in_two, held_z, in_z, final,
    own_sem, wide_send, wide_recv, core_send, core_recv, one_send, one_recv,
    two_send, two_recv, z_send, z_recv, tp_send, tp_recv,
):
    zh, x, y, core, t = place()
    me = ctx_of(zh, x, y, core)
    enter(zh, x, y, core, t)
    sends = []
    sibling = (ctx_of(zh, x, y, 1 - core), t)

    def pieces(i, d, which):
        if i == 0:
            return grad.at[:, (x + d) % X, :, which, i]
        return grad.at[:, :, (y + d) % Y, which, i]

    siblings = {}
    for d in (2, 1, 3, 0):
        for i in range(2):
            copy = remote(
                pieces(i, d, 1 - core), in_core.at[i, d], core_send.at[i, d], core_recv.at[i, d],
                sibling,
            )
            copy.start()
            siblings[i, d] = copy
            sends.append(copy)

    wide, local = [], []
    for i, (ref, out) in enumerate(((att, att_o), (dq, dq_o))):
        for d in (2, 1, 3):
            peer = (t + d) % TP
            copy = remote(
                ref.at[rows_of(peer, MINE), :],
                out.at[:, columns(t, WIDE)],
                wide_send.at[i, d - 1],
                wide_recv.at[i, d - 1],
                (me, peer),
            )
            copy.start()
            wide.append(copy)
            sends.append(copy)
        copy = pltpu.make_async_copy(
            ref.at[rows_of(t, MINE), :], out.at[:, columns(t, WIDE)], own_sem.at[i]
        )
        copy.start()
        local.append(copy)

    def one_peer(i, d):
        if i == 0:
            return (ctx_of(zh, (x + d) % X, y, core), t)
        return (ctx_of(zh, x, (y + d) % Y, core), t)

    firsts = {}
    for d in (2, 1, 3, 0):
        for i in range(2):
            siblings[i, d].wait_recv()

            def add(n, carry):
                a, b = n // 4, n % 4
                if i == 0:
                    mine = grad[a, (x + d) % X, b, core, i]
                else:
                    mine = grad[a, b, (y + d) % Y, core, i]
                held[i, d, a, b] = (mine.astype(f32) + in_core[i, d, a, b].astype(f32)).astype(bf16)
                return carry

            lax.fori_loop(0, 8, add, 0)
            if d > 0:
                copy = remote(
                    held.at[i, d], in_one.at[i, d - 1], one_send.at[i, d - 1],
                    one_recv.at[i, d - 1], one_peer(i, d),
                )
                copy.start()
                firsts[i, d] = copy
                sends.append(copy)

    seconds = {}
    for i in range(2):
        for d in (1, 3, 2):
            firsts[i, d].wait_recv()
        at = y if i == 0 else x
        for e in (2, 1, 3, 0):
            b = (at + e) % 4
            for a in range(2):
                total = held[i, 0, a, b].astype(f32)
                for d in range(3):
                    total = total + in_one[i, d, a, b].astype(f32)
                held_two[i, e, a] = total.astype(bf16)
            if e > 0:
                copy = remote(
                    held_two.at[i, e], in_two.at[i, e - 1], two_send.at[i, e - 1],
                    two_recv.at[i, e - 1], one_peer(1 - i, e),
                )
                copy.start()
                seconds[i, e] = copy
                sends.append(copy)

    across = []
    for i in range(2):
        for e in (1, 3, 2):
            seconds[i, e].wait_recv()
        for a in range(2):
            total = held_two[i, 0, a].astype(f32)
            for e in range(3):
                total = total + in_two[i, e, a].astype(f32)
            held_z[i, a] = total.astype(bf16)
        copy = remote(
            held_z.at[i, 1 - zh], in_z.at[i], z_send.at[i], z_recv.at[i],
            (ctx_of(1 - zh, x, y, core), t),
        )
        copy.start()
        across.append(copy)
        sends.append(copy)

    small = []
    for i, out in enumerate((dk_o, dv_o)):
        across[i].wait_recv()
        final[i] = (held_z[i, zh].astype(f32) + in_z[i].astype(f32)).astype(bf16)
        for d in (2, 1, 3):
            peer = (t + d) % TP
            copy = remote(
                final.at[i, rows_of(peer, MINE), :],
                out.at[:, columns(t, HEAD)],
                tp_send.at[i, d - 1],
                tp_recv.at[i, d - 1],
                (me, peer),
            )
            copy.start()
            small.append(copy)
            sends.append(copy)
        copy = pltpu.make_async_copy(
            final.at[i, rows_of(t, MINE), :], out.at[:, columns(t, HEAD)], own_sem.at[2 + i]
        )
        copy.start()
        local.append(copy)
    for copy in small + wide:
        copy.wait_recv()
    for copy in local:
        copy.wait()
    for copy in sends:
        copy.wait_send()


def scatter(att, dq, grad):
    dma = pltpu.SemaphoreType.DMA
    anywhere = pl.BlockSpec(memory_space=pl.ANY)
    vmem = pl.BlockSpec(memory_space=pltpu.VMEM)
    grad = grad.reshape(ZH, X, Y, CORE, 2, ROWS, HEAD)
    return pl.pallas_call(
        scatter_kernel,
        out_shape=(
            jax.ShapeDtypeStruct((MINE, TP * WIDE), bf16),
            jax.ShapeDtypeStruct((MINE, TP * WIDE), bf16),
            jax.ShapeDtypeStruct((MINE, TP * HEAD), bf16),
            jax.ShapeDtypeStruct((MINE, TP * HEAD), bf16),
        ),
        in_specs=[anywhere, anywhere, vmem],
        out_specs=[anywhere] * 4,
        scratch_shapes=[
            pltpu.VMEM((2, 4, ZH, 4, ROWS, HEAD), bf16),
            pltpu.VMEM((2, 4, ZH, 4, ROWS, HEAD), bf16),
            pltpu.VMEM((2, 3, ZH, 4, ROWS, HEAD), bf16),
            pltpu.VMEM((2, 4, ZH, ROWS, HEAD), bf16),
            pltpu.VMEM((2, 3, ZH, ROWS, HEAD), bf16),
            pltpu.VMEM((2, ZH, ROWS, HEAD), bf16),
            pltpu.VMEM((2, ROWS, HEAD), bf16),
            pltpu.VMEM((2, ROWS, HEAD), bf16),
            dma((4,)),
            dma((2, 3)), dma((2, 3)),
            dma((2, 4)), dma((2, 4)),
            dma((2, 3)), dma((2, 3)),
            dma((2, 3)), dma((2, 3)),
            dma((2,)), dma((2,)),
            dma((2, 3)), dma((2, 3)),
        ],
        compiler_params=pltpu.CompilerParams(
            collective_id=1, has_side_effects=True, vmem_limit_bytes=VMEM_LIMIT
        ),
        name="scatter",
    )(att, dq, grad)


def per_device(queries, keys, values, out_grad, doc_lengths, row_block):
    q, g, kv = gather(queries, keys, values, out_grad)
    att, dq, grad = attend(doc_lengths, row_block, q, g, kv)
    return scatter(att, dq, grad)


def solution(mesh):
    return jax.shard_map(
        per_device,
        mesh=mesh,
        in_specs=(P(("ctx", "tp"), None),) * 4 + (P(), P()),
        out_specs=(P(("ctx", "tp"), None),) * 4,
        check_vma=False,
    )
```

```python
import math

import jax
import jax.numpy as jnp
from jax import lax
from jax.experimental import pallas as pl
from jax.experimental.pallas import tpu as pltpu
from jax.sharding import PartitionSpec as P

HEAD = 128
BLOCK = 64
GROUP = 8
DOCS = 16
NBLK = 128
ZH, X, Y, CORE, TP = 2, 4, 4, 2, 4
ROWS = 2 * BLOCK
MINE = ROWS // TP
WIDE = GROUP * HEAD
TILE = 256
BACK = 2048 // BLOCK
WINDOW = (BACK + 1) * BLOCK
TILES = BACK * BLOCK // TILE
LANES = GROUP * BLOCK
SCALE = 1.0 / math.sqrt(HEAD)
SCALE2 = SCALE * math.log2(math.e)
NEGATIVE = -1e30
VMEM_LIMIT = 56 * 1024 * 1024
f32 = jnp.float32
bf16 = jnp.bfloat16


def place():
    c = lax.axis_index("ctx")
    t = lax.axis_index("tp")
    return c // 32, (c // 8) % 4, (c // 2) % 4, c % 2, t


def ctx_of(zh, x, y, core):
    return ((zh * X + x) * Y + y) * CORE + core


def enter(me, t, zh, x, y, core):
    barrier = pltpu.get_barrier_semaphore()
    peers = near(zh, x, y, core, t)
    peers += [(ctx_of(zh, (x + d) % X, y, core), t) for d in range(1, X)]
    peers += [(ctx_of(zh, x, (y + d) % Y, core), t) for d in range(1, Y)]
    peers += [(ctx_of(zh, x, y, 1 - core), t)]
    for peer in peers:
        pl.semaphore_signal(barrier, inc=1, device_id=peer, device_id_type=pl.DeviceIdType.MESH)
    pl.semaphore_wait(barrier, len(peers))


def near(zh, x, y, core, t):
    return [
        (ctx_of((zh + a) % ZH, x, y, core), (t + d) % TP)
        for a in range(ZH)
        for d in range(TP)
        if a + d > 0
    ]


def remote(src, dst, send, recv, peer):
    return pltpu.make_async_remote_copy(
        src_ref=src,
        dst_ref=dst,
        send_sem=send,
        recv_sem=recv,
        device_id=peer,
        device_id_type=pl.DeviceIdType.MESH,
    )


def columns(index, width):
    return pl.ds(pl.multiple_of(index * width, width), width)


def rows_of(index, count):
    return pl.ds(pl.multiple_of(index * count, count), count)


def mm(a, b, ca, cb):
    return lax.dot_general(a, b, (((ca,), (cb,)), ((), ())), preferred_element_type=f32)


def fused_kernel(
    doc, row_block, slot_of, q, k, v, g, att_o, dq_o, dk_o, dv_o,
    kbuf, vbuf, q_in, g_in, kwin, vwin, qh, gh, qs, gs, s_scr, w_scr, dk_rel, dv_rel,
    out_core, in_core, held, in_one, held_two, in_two, held_z, in_fin,
    own_sem, tp_send, tp_recv, wide_send, wide_recv, one_send, one_recv, two_send, two_recv,
    core_send, core_recv, res_send, res_recv, r0_send, r0_recv, r1_send, r1_recv,
    r2_send, r2_recv, r3_send, r3_recv,
):
    zh, x, y, core, t = place()
    c = lax.axis_index("ctx")
    enter(c, t, zh, x, y, core)
    peers = near(zh, x, y, core, t)
    sibling = (ctx_of(zh, x, y, 1 - core), t)
    sends = []

    def go(copy):
        copy.start()
        sends.append(copy)
        return copy

    def x_peer(d):
        return (ctx_of(zh, (x + d) % X, y, core), t)

    def y_peer(d):
        return (ctx_of(zh, x, (y + d) % Y, core), t)

    bufs = (kbuf, vbuf)

    mine = pl.ds(pl.multiple_of((t % 2) * MINE, MINE), MINE)
    small = []
    for n, peer in enumerate(peers):
        for i, ref in enumerate((k, v)):
            small.append(go(remote(
                ref.at[:, columns(peer[1], HEAD)],
                bufs[i].at[zh, x, y, core, t // 2, mine, :],
                tp_send.at[n, i], tp_recv.at[n, i], peer,
            )))
    local = []
    for i, ref in enumerate((k, v)):
        local.append(pltpu.make_async_copy(
            ref.at[:, columns(t, HEAD)], bufs[i].at[zh, x, y, core, t // 2, mine, :], own_sem.at[i]
        ))
    for i, (ref, to) in enumerate(((q, q_in), (g, g_in))):
        local.append(pltpu.make_async_copy(
            ref.at[:, columns(t, WIDE)], to.at[rows_of(t, MINE), :], own_sem.at[2 + i]
        ))
    for copy in local:
        copy.start()

    for copy in small:
        copy.wait_recv()
    local[0].wait()
    local[1].wait()

    def chunk(i, dx, dy):
        return bufs[i].at[:, (x + dx) % X, (y + dy) % Y, core]

    firsts = {}
    for d in (2, 1, 3):
        for i in range(2):
            here = chunk(i, 0, 0)
            firsts[i, d] = go(remote(
                here, here, one_send.at[i, d - 1], one_recv.at[i, d - 1],
                x_peer(d) if i == 0 else y_peer(d),
            ))

    wide = []
    for i, (ref, to) in enumerate(((q, q_in), (g, g_in))):
        for d in (2, 1, 3):
            peer = (t + d) % TP
            wide.append(go(remote(
                ref.at[:, columns(peer, WIDE)], to.at[rows_of(t, MINE), :],
                wide_send.at[i, d - 1], wide_recv.at[i, d - 1], (c, peer),
            )))

    seconds = {}
    siblings = []

    def to_sibling(i, d, e):
        dx, dy = (-d, -e) if i == 0 else (-e, -d)
        here = chunk(i, dx, dy)
        siblings.append(go(remote(
            here, here, core_send.at[i, d, e], core_recv.at[i, d, e], sibling
        )))

    def spread(i, d):
        dx, dy = (-d, 0) if i == 0 else (0, -d)
        here = chunk(i, dx, dy)
        for e in (2, 1, 3):
            seconds[i, d, e] = go(remote(
                here, here, two_send.at[i, d, e - 1], two_recv.at[i, d, e - 1],
                y_peer(e) if i == 0 else x_peer(e),
            ))
        to_sibling(i, d, 0)

    spread(0, 0)
    spread(1, 0)
    for d in (1, 3, 2):
        for i in range(2):
            firsts[i, d].wait_recv()
            spread(i, d)
    for d in (0, 1, 3, 2):
        for e in (1, 3, 2):
            for i in range(2):
                seconds[i, d, e].wait_recv()
                to_sibling(i, d, e)

    for copy in wide:
        copy.wait_recv()
    local[2].wait()
    local[3].wait()
    for b in range(2):
        here = pl.ds(b * BLOCK, BLOCK)
        for h in range(GROUP):
            qh[b, pl.ds(h * BLOCK, BLOCK), :] = q_in[here, pl.ds(h * HEAD, HEAD)]
            gh[b, pl.ds(h * BLOCK, BLOCK), :] = g_in[here, pl.ds(h * HEAD, HEAD)]

    offset = lax.broadcasted_iota(jnp.int32, (1, LANES), 1) % BLOCK
    base, low = [], []
    for b in range(2):
        block = row_block[2 * c + b]
        position = block * BLOCK + offset
        lowest = jnp.zeros((1, LANES), jnp.int32)
        end = jnp.int32(0)
        for d in range(DOCS):
            end = end + doc[d]
            lowest = jnp.where(position >= end, end, lowest)
        base.append(block - BACK)
        low.append(lowest - (block - BACK) * BLOCK)

    for copy in siblings:
        copy.wait_recv()

    def window(j, carry):
        to = pl.ds(pl.multiple_of(j * BLOCK, BLOCK), BLOCK)
        for b in range(2):
            s = slot_of[jnp.maximum(base[b] + j, 0)]
            at = tuple(lax.rem(lax.div(s, n), m) for n, m in ((64, 2), (16, 4), (4, 4), (2, 2), (1, 2)))
            kwin[b, to, :] = kbuf[at]
            vwin[b, to, :] = vbuf[at]
        return carry

    lax.fori_loop(0, BACK + 1, window, 0)

    def keys_of(tile):
        return pl.ds(pl.multiple_of(tile * TILE, TILE), TILE)

    tail = pl.ds(BACK * BLOCK, BLOCK)
    at_tile = lax.broadcasted_iota(jnp.int32, (TILE, LANES), 0)
    at_tail = lax.broadcasted_iota(jnp.int32, (BLOCK, LANES), 0)

    def folded(values, fold):
        return fold(values.reshape(values.shape[0] // 8, 8, LANES), axis=0)

    def scores(tile, tops):
        out = []
        for b in range(2):
            s = mm(kwin[b, keys_of(tile), :], qh[b], 1, 1)
            s = jnp.where(at_tile >= low[b] - tile * TILE, s, NEGATIVE)
            s_scr[b, keys_of(tile), :] = s
            out.append(jnp.maximum(tops[b], folded(s, jnp.max)))
        return tuple(out)

    tops = []
    for b in range(2):
        s = mm(kwin[b, tail, :], qh[b], 1, 1)
        seen = (at_tail >= low[b] - BACK * BLOCK) & (at_tail <= offset)
        s = jnp.where(seen, s, NEGATIVE)
        s_scr[b, tail, :] = s
        tops.append(folded(s, jnp.max))
    tops = lax.fori_loop(0, TILES, scores, tuple(tops))
    tops = [jnp.max(top, axis=0, keepdims=True) for top in tops]

    def weigh_part(b, part, total, acc):
        w = jnp.exp2((s_scr[b, part, :] - tops[b]) * SCALE2)
        total = total + folded(w, jnp.sum)
        w16 = w.astype(bf16)
        w_scr[b, part, :] = w16
        return total, acc + mm(vwin[b, part, :], w16, 0, 0)

    def weigh(tile, state):
        out = [weigh_part(b, keys_of(tile), *state[b]) for b in range(2)]
        return tuple(out)

    state = tuple(
        weigh_part(b, tail, jnp.zeros((8, LANES), f32), jnp.zeros((HEAD, LANES), f32))
        for b in range(2)
    )
    state = lax.fori_loop(0, TILES, weigh, state)

    inverse, delta = [], []
    results = []

    for b in range(2):
        total, acc = state[b]
        inv = 1.0 / jnp.sum(total, axis=0, keepdims=True)
        att_t = acc * inv
        g_t = gh[b].astype(f32).T
        delta.append(jnp.sum(g_t * att_t, axis=0, keepdims=True))
        inverse.append(inv)
        att = att_t.T.astype(bf16)
        inv_rows = jnp.broadcast_to(inv, (HEAD, LANES)).T
        gs[b] = (gh[b].astype(f32) * inv_rows).astype(bf16)
        qs[b] = (qh[b].astype(f32) * (inv_rows * SCALE)).astype(bf16)
        for h in range(GROUP):
            q_in[pl.ds(b * BLOCK, BLOCK), pl.ds(h * HEAD, HEAD)] = att[h * BLOCK : (h + 1) * BLOCK]

    def send_rows(i, ref, out):
        for d in (2, 1, 3):
            peer = (t + d) % TP
            results.append(go(remote(
                ref.at[rows_of(peer, MINE), :], out.at[:, columns(t, WIDE)],
                res_send.at[i, d - 1], res_recv.at[i, d - 1], (c, peer),
            )))
        copy = pltpu.make_async_copy(
            ref.at[rows_of(t, MINE), :], out.at[:, columns(t, WIDE)], own_sem.at[5 + i]
        )
        copy.start()
        local.append(copy)

    send_rows(0, q_in, att_o)

    def back_part(b, part, first, dq_t):
        keys = kwin[b, part, :]
        dp = mm(vwin[b, part, :], gh[b], 1, 1)
        w16 = w_scr[b, part, :]
        ds = (w16.astype(f32) * (dp - delta[b])).astype(bf16)
        to = pl.ds(first + 1, w16.shape[0] // BLOCK)
        dk_rel[b, to] = mm(ds, qs[b], 1, 0).reshape(-1, BLOCK, HEAD)
        dv_rel[b, to] = mm(w16, gs[b], 1, 0).reshape(-1, BLOCK, HEAD)
        return dq_t + mm(keys, ds, 0, 0)

    def back(tile, state):
        return tuple(back_part(b, keys_of(tile), tile * (TILE // BLOCK), state[b]) for b in range(2))

    dqs = tuple(back_part(b, tail, BACK, jnp.zeros((HEAD, LANES), f32)) for b in range(2))
    dqs = lax.fori_loop(0, TILES, back, dqs)
    for b in range(2):
        dq = (dqs[b] * (inverse[b] * SCALE)).T.astype(bf16)
        for h in range(GROUP):
            g_in[pl.ds(b * BLOCK, BLOCK), pl.ds(h * HEAD, HEAD)] = dq[h * BLOCK : (h + 1) * BLOCK]

    rels = (dk_rel, dv_rel)
    for ref in rels:
        for b in range(2):
            for zero in (0, BACK + 2):
                ref[b, zero] = jnp.zeros((BLOCK, HEAD), f32)

    def piece(i, d, e, a, which, half):
        dx, dy = (d, e) if i == 0 else (e, d)
        s = ctx_of(a, (x + dx) % X, (y + dy) % Y, which) * 2 + half
        total = None
        for b in range(2):
            rel = row_block[s] - base[b] + 1
            part = rels[i][b, jnp.minimum(jnp.maximum(rel, 0), BACK + 2)]
            total = part if total is None else total + part
        return total

    def one_peer(i, d):
        return x_peer(d) if i == 0 else y_peer(d)

    order = [(d, i) for d in (2, 1, 3, 0) for i in range(2)]
    r0 = {}
    for d, i in order:
        def assemble(e, carry):
            for a in range(ZH):
                for half in range(2):
                    out_core[i, d, e, a, half] = piece(i, d, e, a, 1 - core, half).astype(bf16)
            return carry

        lax.fori_loop(0, 4, assemble, 0)
        r0[i, d] = go(remote(
            out_core.at[i, d], in_core.at[i, d], r0_send.at[i, d], r0_recv.at[i, d], sibling
        ))
    send_rows(1, g_in, dq_o)

    def r1(i, d, e):
        return remote(
            held.at[i, d, e], in_one.at[i, d - 1, e], r1_send.at[i, d - 1, e],
            r1_recv.at[i, d - 1, e], one_peer(i, d),
        )

    for d, i in order:
        r0[i, d].wait_recv()

        def add(n, carry):
            e = (n + 1) % 4
            for a in range(ZH):
                for half in range(2):
                    total = piece(i, d, e, a, core, half) + in_core[i, d, e, a, half].astype(f32)
                    held[i, d, e, a, half] = total.astype(bf16)
            if d > 0:
                r1(i, d, e).start()
            return carry

        lax.fori_loop(0, 4, add, 0)

    def r2(i, e):
        return remote(
            held_two.at[i, e], in_two.at[i, e - 1], r2_send.at[i, e - 1], r2_recv.at[i, e - 1],
            one_peer(1 - i, e),
        )

    for e in (1, 2, 3, 0):
        for i in range(2):
            for d in (1, 3, 2):
                r1(i, d, e).wait_recv()
            for a in range(ZH):
                total = held[i, 0, e, a].astype(f32)
                for d in range(3):
                    total = total + in_one[i, d, e, a].astype(f32)
                held_two[i, e, a] = total.astype(bf16)
            if e > 0:
                go(r2(i, e))

    last = []
    for i in range(2):
        for e in (1, 2, 3):
            r2(i, e).wait_recv()
        for a in range(ZH):
            total = held_two[i, 0, a].astype(f32)
            for e in range(3):
                total = total + in_two[i, e, a].astype(f32)
            held_z[i, a] = total.astype(bf16)
        for n, peer in enumerate(peers):
            a = (zh + (n + 1) // TP) % ZH
            last.append(go(remote(
                held_z.at[i, a, peer[1] // 2, pl.ds(pl.multiple_of((peer[1] % 2) * MINE, MINE), MINE), :],
                in_fin.at[i, zh, t], r3_send.at[i, n], r3_recv.at[i, n], peer,
            )))
        in_fin[i, zh, t] = held_z[i, zh, t // 2, mine, :]
    for i, out in enumerate((dk_o, dv_o)):
        for n in range(len(peers)):
            last[i * len(peers) + n].wait_recv()
        for h in range(TP):
            total = in_fin[i, 0, h].astype(f32) + in_fin[i, 1, h].astype(f32)
            out[:, pl.ds(h * HEAD, HEAD)] = total.astype(bf16)
    for copy in results:
        copy.wait_recv()
    for copy in local[4:]:
        copy.wait()
    for copy in sends:
        copy.wait_send()
    for i in range(2):
        for d in range(1, 4):
            for e in range(4):
                r1(i, d, e).wait_send()


def fused(doc_lengths, row_block, queries, keys, values, out_grad):
    dma = pltpu.SemaphoreType.DMA
    anywhere = pl.BlockSpec(memory_space=pl.ANY)
    vmem = pl.BlockSpec(memory_space=pltpu.VMEM)
    smem = pl.BlockSpec(memory_space=pltpu.SMEM)
    V = pltpu.VMEM
    slots = (ZH, X, Y, CORE, 2, BLOCK, HEAD)
    piece = (2, BLOCK, HEAD)
    number = jnp.arange(NBLK, dtype=jnp.int32)
    found = row_block[None, :] == number[:, None]
    slot_of = jnp.sum(jnp.where(found, number[None, :], 0), axis=1)
    return pl.pallas_call(
        fused_kernel,
        out_shape=(
            jax.ShapeDtypeStruct((MINE, TP * WIDE), bf16),
            jax.ShapeDtypeStruct((MINE, TP * WIDE), bf16),
            jax.ShapeDtypeStruct((MINE, TP * HEAD), bf16),
            jax.ShapeDtypeStruct((MINE, TP * HEAD), bf16),
        ),
        in_specs=[smem, smem, smem] + [anywhere] * 4,
        out_specs=[anywhere] * 2 + [vmem] * 2,
        scratch_shapes=[
            V(slots, bf16), V(slots, bf16),
            V((ROWS, WIDE), bf16), V((ROWS, WIDE), bf16),
            V((2, WINDOW, HEAD), bf16), V((2, WINDOW, HEAD), bf16),
            V((2, LANES, HEAD), bf16), V((2, LANES, HEAD), bf16),
            V((2, LANES, HEAD), bf16), V((2, LANES, HEAD), bf16),
            V((2, WINDOW, LANES), f32), V((2, WINDOW, LANES), bf16),
            V((2, BACK + 3, BLOCK, HEAD), f32), V((2, BACK + 3, BLOCK, HEAD), f32),
            V((2, 4, 4, ZH) + piece, bf16), V((2, 4, 4, ZH) + piece, bf16),
            V((2, 4, 4, ZH) + piece, bf16), V((2, 3, 4, ZH) + piece, bf16),
            V((2, 4, ZH) + piece, bf16), V((2, 3, ZH) + piece, bf16),
            V((2, ZH) + piece, bf16), V((2, ZH, TP, MINE, HEAD), bf16),
            dma((7,)),
            dma((7, 2)), dma((7, 2)),
            dma((2, 3)), dma((2, 3)),
            dma((2, 3)), dma((2, 3)),
            dma((2, 4, 3)), dma((2, 4, 3)),
            dma((2, 4, 4)), dma((2, 4, 4)),
            dma((2, 3)), dma((2, 3)),
            dma((2, 4)), dma((2, 4)),
            dma((2, 3, 4)), dma((2, 3, 4)),
            dma((2, 3)), dma((2, 3)),
            dma((2, 7)), dma((2, 7)),
        ],
        compiler_params=pltpu.CompilerParams(
            collective_id=0, has_side_effects=True, vmem_limit_bytes=VMEM_LIMIT
        ),
        name="fused",
    )(doc_lengths, row_block, slot_of, queries, keys, values, out_grad)


def hand_over_kernel(*refs):
    held, sems = refs[8:12], refs[12]
    arrive = [pltpu.make_async_copy(refs[i], held[i], sems.at[0, i]) for i in range(4)]
    leave = [pltpu.make_async_copy(held[i], refs[4 + i], sems.at[1, i]) for i in range(4)]
    for copy in arrive:
        copy.start()
    for i in range(4):
        arrive[i].wait()
        leave[i].start()
    for copy in leave:
        copy.wait()


def hand_over(arrays):
    anywhere = pl.BlockSpec(memory_space=pl.ANY)
    return pl.pallas_call(
        hand_over_kernel,
        out_shape=tuple(jax.ShapeDtypeStruct(a.shape, a.dtype) for a in arrays),
        in_specs=[anywhere] * 4,
        out_specs=[anywhere] * 4,
        scratch_shapes=[pltpu.VMEM(a.shape, a.dtype) for a in arrays]
        + [pltpu.SemaphoreType.DMA((2, 4))],
        name="hand_over",
    )(*arrays)


def per_device(queries, keys, values, out_grad, doc_lengths, row_block):
    return hand_over(fused(doc_lengths, row_block, queries, keys, values, out_grad))


def solution(mesh):
    return jax.shard_map(
        per_device,
        mesh=mesh,
        in_specs=(P(("ctx", "tp"), None),) * 4 + (P(), P()),
        out_specs=(P(("ctx", "tp"), None),) * 4,
        check_vma=False,
    )
```

```python
import math

import jax
import jax.numpy as jnp
from jax import lax
from jax.experimental import pallas as pl
from jax.experimental.pallas import tpu as pltpu
from jax.sharding import PartitionSpec as P

HEAD = 128
BLOCK = 64
GROUP = 8
DOCS = 16
NBLK = 128
ZH, X, Y, CORE, TP = 2, 4, 4, 2, 4
ROWS = 2 * BLOCK
MINE = ROWS // TP
WIDE = GROUP * HEAD
TILE = 512
BACK = 2048 // BLOCK
WINDOW = (BACK + 1) * BLOCK
TILES = BACK * BLOCK // TILE
LANES = GROUP * BLOCK
SCALE = 1.0 / math.sqrt(HEAD)
SCALE2 = SCALE * math.log2(math.e)
NEGATIVE = -1e30
VMEM_LIMIT = 56 * 1024 * 1024
f32 = jnp.float32
bf16 = jnp.bfloat16


def place():
    c = lax.axis_index("ctx")
    t = lax.axis_index("tp")
    return c // 32, (c // 8) % 4, (c // 2) % 4, c % 2, t


def ctx_of(zh, x, y, core):
    return ((zh * X + x) * Y + y) * CORE + core


def enter(me, t, zh, x, y, core):
    barrier = pltpu.get_barrier_semaphore()
    peers = near(zh, x, y, core, t)
    peers += [(ctx_of(zh, (x + d) % X, y, core), t) for d in range(1, X)]
    peers += [(ctx_of(zh, x, (y + d) % Y, core), t) for d in range(1, Y)]
    peers += [(ctx_of(zh, x, y, 1 - core), t)]
    for peer in peers:
        pl.semaphore_signal(barrier, inc=1, device_id=peer, device_id_type=pl.DeviceIdType.MESH)
    pl.semaphore_wait(barrier, len(peers))


def near(zh, x, y, core, t):
    return [
        (ctx_of((zh + a) % ZH, x, y, core), (t + d) % TP)
        for a in range(ZH)
        for d in range(TP)
        if a + d > 0
    ]


def remote(src, dst, send, recv, peer):
    return pltpu.make_async_remote_copy(
        src_ref=src,
        dst_ref=dst,
        send_sem=send,
        recv_sem=recv,
        device_id=peer,
        device_id_type=pl.DeviceIdType.MESH,
    )


def columns(index, width):
    return pl.ds(pl.multiple_of(index * width, width), width)


def rows_of(index, count):
    return pl.ds(pl.multiple_of(index * count, count), count)


def mm(a, b, ca, cb):
    return lax.dot_general(a, b, (((ca,), (cb,)), ((), ())), preferred_element_type=f32)


def fused_kernel(
    doc, row_block, slot_of, q, k, v, g, att_o, dq_o, dk_o, dv_o,
    kbuf, vbuf, q_in, g_in, kwin, vwin, qh, gh, qs, gs, s_scr, w_scr, dk_rel, dv_rel,
    out_core, in_core, held, in_one, held_two, in_two, held_z, in_fin,
    own_sem, tp_send, tp_recv, wide_send, wide_recv, one_send, one_recv, two_send, two_recv,
    core_send, core_recv, res_send, res_recv, r0_send, r0_recv, r1_send, r1_recv,
    r2_send, r2_recv, r3_send, r3_recv,
):
    zh, x, y, core, t = place()
    c = lax.axis_index("ctx")
    enter(c, t, zh, x, y, core)
    peers = near(zh, x, y, core, t)
    sibling = (ctx_of(zh, x, y, 1 - core), t)
    sends = []

    def go(copy):
        copy.start()
        sends.append(copy)
        return copy

    def x_peer(d):
        return (ctx_of(zh, (x + d) % X, y, core), t)

    def y_peer(d):
        return (ctx_of(zh, x, (y + d) % Y, core), t)

    bufs = (kbuf, vbuf)

    mine = pl.ds(pl.multiple_of((t % 2) * MINE, MINE), MINE)
    small = []
    for n, peer in enumerate(peers):
        for i, ref in enumerate((k, v)):
            small.append(go(remote(
                ref.at[:, columns(peer[1], HEAD)],
                bufs[i].at[zh, x, y, core, t // 2, mine, :],
                tp_send.at[n, i], tp_recv.at[n, i], peer,
            )))
    local = []
    for i, ref in enumerate((k, v)):
        local.append(pltpu.make_async_copy(
            ref.at[:, columns(t, HEAD)], bufs[i].at[zh, x, y, core, t // 2, mine, :], own_sem.at[i]
        ))
    for i, (ref, to) in enumerate(((q, q_in), (g, g_in))):
        local.append(pltpu.make_async_copy(
            ref.at[:, columns(t, WIDE)], to.at[rows_of(t, MINE), :], own_sem.at[2 + i]
        ))
    for copy in local:
        copy.start()

    for copy in small:
        copy.wait_recv()
    local[0].wait()
    local[1].wait()

    def chunk(i, dx, dy):
        return bufs[i].at[:, (x + dx) % X, (y + dy) % Y, core]

    firsts = {}
    for d in (2, 1, 3):
        for i in range(2):
            here = chunk(i, 0, 0)
            firsts[i, d] = go(remote(
                here, here, one_send.at[i, d - 1], one_recv.at[i, d - 1],
                x_peer(d) if i == 0 else y_peer(d),
            ))

    wide = []
    for i, (ref, to) in enumerate(((q, q_in), (g, g_in))):
        for d in (2, 1, 3):
            peer = (t + d) % TP
            wide.append(go(remote(
                ref.at[:, columns(peer, WIDE)], to.at[rows_of(t, MINE), :],
                wide_send.at[i, d - 1], wide_recv.at[i, d - 1], (c, peer),
            )))

    seconds = {}
    siblings = []

    def to_sibling(i, d, e):
        dx, dy = (-d, -e) if i == 0 else (-e, -d)
        here = chunk(i, dx, dy)
        siblings.append(go(remote(
            here, here, core_send.at[i, d, e], core_recv.at[i, d, e], sibling
        )))

    def spread(i, d):
        dx, dy = (-d, 0) if i == 0 else (0, -d)
        here = chunk(i, dx, dy)
        for e in (2, 1, 3):
            seconds[i, d, e] = go(remote(
                here, here, two_send.at[i, d, e - 1], two_recv.at[i, d, e - 1],
                y_peer(e) if i == 0 else x_peer(e),
            ))
        to_sibling(i, d, 0)

    spread(0, 0)
    spread(1, 0)
    for d in (1, 3, 2):
        for i in range(2):
            firsts[i, d].wait_recv()
            spread(i, d)
    for d in (0, 1, 3, 2):
        for e in (1, 3, 2):
            for i in range(2):
                seconds[i, d, e].wait_recv()
                to_sibling(i, d, e)

    for copy in wide:
        copy.wait_recv()
    local[2].wait()
    local[3].wait()
    for b in range(2):
        here = pl.ds(b * BLOCK, BLOCK)
        for h in range(GROUP):
            qh[b, pl.ds(h * BLOCK, BLOCK), :] = q_in[here, pl.ds(h * HEAD, HEAD)]
            gh[b, pl.ds(h * BLOCK, BLOCK), :] = g_in[here, pl.ds(h * HEAD, HEAD)]

    offset = lax.broadcasted_iota(jnp.int32, (1, LANES), 1) % BLOCK
    base, low = [], []
    for b in range(2):
        block = row_block[2 * c + b]
        position = block * BLOCK + offset
        lowest = jnp.zeros((1, LANES), jnp.int32)
        end = jnp.int32(0)
        for d in range(DOCS):
            end = end + doc[d]
            lowest = jnp.where(position >= end, end, lowest)
        base.append(block - BACK)
        low.append(lowest - (block - BACK) * BLOCK)

    for copy in siblings:
        copy.wait_recv()

    def window(j, carry):
        to = pl.ds(pl.multiple_of(j * BLOCK, BLOCK), BLOCK)
        for b in range(2):
            s = slot_of[jnp.maximum(base[b] + j, 0)]
            at = tuple(lax.rem(lax.div(s, n), m) for n, m in ((64, 2), (16, 4), (4, 4), (2, 2), (1, 2)))
            kwin[b, to, :] = kbuf[at]
            vwin[b, to, :] = vbuf[at]
        return carry

    lax.fori_loop(0, BACK + 1, window, 0)

    def keys_of(tile):
        return pl.ds(pl.multiple_of(tile * TILE, TILE), TILE)

    tail = pl.ds(BACK * BLOCK, BLOCK)
    at_tile = lax.broadcasted_iota(jnp.int32, (TILE, LANES), 0)
    at_tail = lax.broadcasted_iota(jnp.int32, (BLOCK, LANES), 0)

    def folded(values, fold):
        return fold(values.reshape(values.shape[0] // 8, 8, LANES), axis=0)

    def scores(tile, tops):
        out = []
        for b in range(2):
            s = mm(kwin[b, keys_of(tile), :], qh[b], 1, 1)
            s = jnp.where(at_tile >= low[b] - tile * TILE, s, NEGATIVE)
            s_scr[b, keys_of(tile), :] = s
            out.append(jnp.maximum(tops[b], folded(s, jnp.max)))
        return tuple(out)

    tops = []
    for b in range(2):
        s = mm(kwin[b, tail, :], qh[b], 1, 1)
        seen = (at_tail >= low[b] - BACK * BLOCK) & (at_tail <= offset)
        s = jnp.where(seen, s, NEGATIVE)
        s_scr[b, tail, :] = s
        tops.append(folded(s, jnp.max))
    tops = lax.fori_loop(0, TILES, scores, tuple(tops), unroll=TILES)
    tops = [jnp.max(top, axis=0, keepdims=True) for top in tops]

    def weigh_part(b, part, total, acc):
        w = jnp.exp2((s_scr[b, part, :] - tops[b]) * SCALE2)
        total = total + folded(w, jnp.sum)
        w16 = w.astype(bf16)
        w_scr[b, part, :] = w16
        return total, acc + mm(vwin[b, part, :], w16, 0, 0)

    def weigh(tile, state):
        out = [weigh_part(b, keys_of(tile), *state[b]) for b in range(2)]
        return tuple(out)

    state = tuple(
        weigh_part(b, tail, jnp.zeros((8, LANES), f32), jnp.zeros((HEAD, LANES), f32))
        for b in range(2)
    )
    state = lax.fori_loop(0, TILES, weigh, state, unroll=TILES)

    inverse, delta = [], []
    results = []

    for b in range(2):
        total, acc = state[b]
        inv = 1.0 / jnp.sum(total, axis=0, keepdims=True)
        att_t = acc * inv
        g_t = gh[b].astype(f32).T
        delta.append(jnp.sum(g_t * att_t, axis=0, keepdims=True))
        inverse.append(inv)
        att = att_t.T.astype(bf16)
        inv_rows = jnp.broadcast_to(inv, (HEAD, LANES)).T
        gs[b] = (gh[b].astype(f32) * inv_rows).astype(bf16)
        qs[b] = (qh[b].astype(f32) * (inv_rows * SCALE)).astype(bf16)
        for h in range(GROUP):
            q_in[pl.ds(b * BLOCK, BLOCK), pl.ds(h * HEAD, HEAD)] = att[h * BLOCK : (h + 1) * BLOCK]

    def send_rows(i, ref, out):
        for d in (2, 1, 3):
            peer = (t + d) % TP
            results.append(go(remote(
                ref.at[rows_of(peer, MINE), :], out.at[:, columns(t, WIDE)],
                res_send.at[i, d - 1], res_recv.at[i, d - 1], (c, peer),
            )))
        copy = pltpu.make_async_copy(
            ref.at[rows_of(t, MINE), :], out.at[:, columns(t, WIDE)], own_sem.at[5 + i]
        )
        copy.start()
        local.append(copy)

    send_rows(0, q_in, att_o)

    def value_part(b, part, first):
        dv = mm(w_scr[b, part, :], gs[b], 1, 0)
        dv_rel[b, pl.ds(first + 1, dv.shape[0] // BLOCK)] = dv.reshape(-1, BLOCK, HEAD)

    def value_tile(tile, carry):
        for b in range(2):
            value_part(b, keys_of(tile), tile * (TILE // BLOCK))
        return carry

    for b in range(2):
        value_part(b, tail, BACK)
    lax.fori_loop(0, TILES, value_tile, 0, unroll=TILES)

    rels = (dk_rel, dv_rel)
    for ref in rels:
        for b in range(2):
            for zero in (0, BACK + 2):
                ref[b, zero] = jnp.zeros((BLOCK, HEAD), f32)

    def piece(i, f, d, e, a, which):
        dx, dy = (d, e) if f == 0 else (e, d)
        s = ctx_of(a, (x + dx) % X, (y + dy) % Y, which) * 2 + f
        total = None
        for b in range(2):
            rel = row_block[s] - base[b] + 1
            part = rels[i][b, jnp.minimum(jnp.maximum(rel, 0), BACK + 2)]
            total = part if total is None else total + part
        return total

    def one_peer(f, d):
        return x_peer(d) if f == 0 else y_peer(d)

    order = [(d, f) for d in (2, 1, 3, 0) for f in range(2)]
    r0 = {}

    def assemble(i):
        for d, f in order:
            def fill(e, carry):
                for a in range(ZH):
                    out_core[i, f, d, e, a] = piece(i, f, d, e, a, 1 - core).astype(bf16)
                return carry

            lax.fori_loop(0, 4, fill, 0)
            r0[i, f, d] = go(remote(
                out_core.at[i, f, d], in_core.at[i, f, d],
                r0_send.at[i, f, d], r0_recv.at[i, f, d], sibling,
            ))

    def r1(i, f, d, e):
        return remote(
            held.at[i, f, d, e], in_one.at[i, f, d - 1, e], r1_send.at[i, f, d - 1, e],
            r1_recv.at[i, f, d - 1, e], one_peer(f, d),
        )

    def join(i):
        for d, f in order:
            r0[i, f, d].wait_recv()

            def add(n, carry):
                e = (n + 1) % 4
                for a in range(ZH):
                    total = piece(i, f, d, e, a, core) + in_core[i, f, d, e, a].astype(f32)
                    held[i, f, d, e, a] = total.astype(bf16)
                if d > 0:
                    r1(i, f, d, e).start()
                return carry

            lax.fori_loop(0, 4, add, 0)

    def back_part(b, part, first, dq_t):
        keys = kwin[b, part, :]
        dp = mm(vwin[b, part, :], gh[b], 1, 1)
        ds = (w_scr[b, part, :].astype(f32) * (dp - delta[b])).astype(bf16)
        dk = mm(ds, qs[b], 1, 0)
        dk_rel[b, pl.ds(first + 1, dk.shape[0] // BLOCK)] = dk.reshape(-1, BLOCK, HEAD)
        return dq_t + mm(keys, ds, 0, 0)

    def back(b):
        def step(tile, dq_t):
            return back_part(b, keys_of(tile), tile * (TILE // BLOCK), dq_t)

        dq_t = back_part(b, tail, BACK, jnp.zeros((HEAD, LANES), f32))
        dq_t = lax.fori_loop(0, TILES, step, dq_t, unroll=TILES)
        dq = (dq_t * (inverse[b] * SCALE)).T.astype(bf16)
        for h in range(GROUP):
            g_in[pl.ds(b * BLOCK, BLOCK), pl.ds(h * HEAD, HEAD)] = dq[h * BLOCK : (h + 1) * BLOCK]

    assemble(1)
    back(0)
    join(1)
    back(1)
    assemble(0)
    send_rows(1, g_in, dq_o)
    join(0)

    def r2(i, f, e):
        return remote(
            held_two.at[i, f, e], in_two.at[i, f, e - 1], r2_send.at[i, f, e - 1],
            r2_recv.at[i, f, e - 1], one_peer(1 - f, e),
        )

    for i in (1, 0):
        for e in (1, 2, 3, 0):
            for f in range(2):
                for d in (1, 3, 2):
                    r1(i, f, d, e).wait_recv()
                for a in range(ZH):
                    total = held[i, f, 0, e, a].astype(f32)
                    for d in range(3):
                        total = total + in_one[i, f, d, e, a].astype(f32)
                    held_two[i, f, e, a] = total.astype(bf16)
                if e > 0:
                    go(r2(i, f, e))

    last = {}
    for i in (1, 0):
        for f in range(2):
            for e in (1, 2, 3):
                r2(i, f, e).wait_recv()
            for a in range(ZH):
                total = held_two[i, f, 0, a].astype(f32)
                for e in range(3):
                    total = total + in_two[i, f, e, a].astype(f32)
                held_z[i, a, f] = total.astype(bf16)
        for n, peer in enumerate(peers):
            a = (zh + (n + 1) // TP) % ZH
            last[i, n] = go(remote(
                held_z.at[i, a, peer[1] // 2, pl.ds(pl.multiple_of((peer[1] % 2) * MINE, MINE), MINE), :],
                in_fin.at[i, zh, t], r3_send.at[i, n], r3_recv.at[i, n], peer,
            ))
        in_fin[i, zh, t] = held_z[i, zh, t // 2, mine, :]
    for i, out in ((1, dv_o), (0, dk_o)):
        for n in range(len(peers)):
            last[i, n].wait_recv()
        for h in range(TP):
            total = in_fin[i, 0, h].astype(f32) + in_fin[i, 1, h].astype(f32)
            out[:, pl.ds(h * HEAD, HEAD)] = total.astype(bf16)
    for copy in results:
        copy.wait_recv()
    for copy in local[4:]:
        copy.wait()
    for copy in sends:
        copy.wait_send()
    for i in range(2):
        for f in range(2):
            for d in range(1, 4):
                for e in range(4):
                    r1(i, f, d, e).wait_send()


def fused(doc_lengths, row_block, queries, keys, values, out_grad):
    dma = pltpu.SemaphoreType.DMA
    anywhere = pl.BlockSpec(memory_space=pl.ANY)
    vmem = pl.BlockSpec(memory_space=pltpu.VMEM)
    smem = pl.BlockSpec(memory_space=pltpu.SMEM)
    V = pltpu.VMEM
    slots = (ZH, X, Y, CORE, 2, BLOCK, HEAD)
    piece = (BLOCK, HEAD)
    number = jnp.arange(NBLK, dtype=jnp.int32)
    found = row_block[None, :] == number[:, None]
    slot_of = jnp.sum(jnp.where(found, number[None, :], 0), axis=1)
    return pl.pallas_call(
        fused_kernel,
        out_shape=(
            jax.ShapeDtypeStruct((MINE, TP * WIDE), bf16),
            jax.ShapeDtypeStruct((MINE, TP * WIDE), bf16),
            jax.ShapeDtypeStruct((MINE, TP * HEAD), bf16),
            jax.ShapeDtypeStruct((MINE, TP * HEAD), bf16),
        ),
        in_specs=[smem, smem, smem] + [anywhere] * 4,
        out_specs=[anywhere] * 2 + [vmem] * 2,
        scratch_shapes=[
            V(slots, bf16), V(slots, bf16),
            V((ROWS, WIDE), bf16), V((ROWS, WIDE), bf16),
            V((2, WINDOW, HEAD), bf16), V((2, WINDOW, HEAD), bf16),
            V((2, LANES, HEAD), bf16), V((2, LANES, HEAD), bf16),
            V((2, LANES, HEAD), bf16), V((2, LANES, HEAD), bf16),
            V((2, WINDOW, LANES), f32), V((2, WINDOW, LANES), bf16),
            V((2, BACK + 3, BLOCK, HEAD), f32), V((2, BACK + 3, BLOCK, HEAD), f32),
            V((2, 2, 4, 4, ZH) + piece, bf16), V((2, 2, 4, 4, ZH) + piece, bf16),
            V((2, 2, 4, 4, ZH) + piece, bf16), V((2, 2, 3, 4, ZH) + piece, bf16),
            V((2, 2, 4, ZH) + piece, bf16), V((2, 2, 3, ZH) + piece, bf16),
            V((2, ZH, 2) + piece, bf16), V((2, ZH, TP, MINE, HEAD), bf16),
            dma((7,)),
            dma((7, 2)), dma((7, 2)),
            dma((2, 3)), dma((2, 3)),
            dma((2, 3)), dma((2, 3)),
            dma((2, 4, 3)), dma((2, 4, 3)),
            dma((2, 4, 4)), dma((2, 4, 4)),
            dma((2, 3)), dma((2, 3)),
            dma((2, 2, 4)), dma((2, 2, 4)),
            dma((2, 2, 3, 4)), dma((2, 2, 3, 4)),
            dma((2, 2, 3)), dma((2, 2, 3)),
            dma((2, 7)), dma((2, 7)),
        ],
        compiler_params=pltpu.CompilerParams(
            collective_id=0, has_side_effects=True, vmem_limit_bytes=VMEM_LIMIT
        ),
        name="fused",
    )(doc_lengths, row_block, slot_of, queries, keys, values, out_grad)


def hand_over_kernel(*refs):
    held, sems = refs[8:12], refs[12]
    arrive = [pltpu.make_async_copy(refs[i], held[i], sems.at[0, i]) for i in range(4)]
    leave = [pltpu.make_async_copy(held[i], refs[4 + i], sems.at[1, i]) for i in range(4)]
    for copy in arrive:
        copy.start()
    for i in range(4):
        arrive[i].wait()
        leave[i].start()
    for copy in leave:
        copy.wait()


def hand_over(arrays):
    anywhere = pl.BlockSpec(memory_space=pl.ANY)
    return pl.pallas_call(
        hand_over_kernel,
        out_shape=tuple(jax.ShapeDtypeStruct(a.shape, a.dtype) for a in arrays),
        in_specs=[anywhere] * 4,
        out_specs=[anywhere] * 4,
        scratch_shapes=[pltpu.VMEM(a.shape, a.dtype) for a in arrays]
        + [pltpu.SemaphoreType.DMA((2, 4))],
        name="hand_over",
    )(*arrays)


def per_device(queries, keys, values, out_grad, doc_lengths, row_block):
    return hand_over(fused(doc_lengths, row_block, queries, keys, values, out_grad))


def solution(mesh):
    return jax.shard_map(
        per_device,
        mesh=mesh,
        in_specs=(P(("ctx", "tp"), None),) * 4 + (P(), P()),
        out_specs=(P(("ctx", "tp"), None),) * 4,
        check_vma=False,
    )
```

```python
import math

import jax
import jax.numpy as jnp
from jax import lax
from jax.experimental import pallas as pl
from jax.experimental.pallas import tpu as pltpu
from jax.sharding import PartitionSpec as P

HEAD = 128
BLOCK = 64
GROUP = 8
DOCS = 16
NBLK = 128
ZH, X, Y, CORE, TP = 2, 4, 4, 2, 4
ROWS = 2 * BLOCK
MINE = ROWS // TP
WIDE = GROUP * HEAD
TILE = 512
BACK = 2048 // BLOCK
WINDOW = (BACK + 1) * BLOCK
TILES = BACK * BLOCK // TILE
LANES = GROUP * BLOCK
SCALE = 1.0 / math.sqrt(HEAD)
SCALE2 = SCALE * math.log2(math.e)
NEGATIVE = -1e30
VMEM_LIMIT = 56 * 1024 * 1024
f32 = jnp.float32
bf16 = jnp.bfloat16


def place():
    c = lax.axis_index("ctx")
    t = lax.axis_index("tp")
    return c // 32, (c // 8) % 4, (c // 2) % 4, c % 2, t


def ctx_of(zh, x, y, core):
    return ((zh * X + x) * Y + y) * CORE + core


def enter(me, t, zh, x, y, core):
    barrier = pltpu.get_barrier_semaphore()
    peers = near(zh, x, y, core, t)
    peers += [(ctx_of(zh, (x + d) % X, y, core), t) for d in range(1, X)]
    peers += [(ctx_of(zh, x, (y + d) % Y, core), t) for d in range(1, Y)]
    peers += [(ctx_of(zh, x, y, 1 - core), t)]
    for peer in peers:
        pl.semaphore_signal(barrier, inc=1, device_id=peer, device_id_type=pl.DeviceIdType.MESH)
    pl.semaphore_wait(barrier, len(peers))


def near(zh, x, y, core, t):
    return [
        (ctx_of((zh + a) % ZH, x, y, core), (t + d) % TP)
        for a in range(ZH)
        for d in range(TP)
        if a + d > 0
    ]


def remote(src, dst, send, recv, peer):
    return pltpu.make_async_remote_copy(
        src_ref=src,
        dst_ref=dst,
        send_sem=send,
        recv_sem=recv,
        device_id=peer,
        device_id_type=pl.DeviceIdType.MESH,
    )


def columns(index, width):
    return pl.ds(pl.multiple_of(index * width, width), width)


def rows_of(index, count):
    return pl.ds(pl.multiple_of(index * count, count), count)


def mm(a, b, ca, cb):
    return lax.dot_general(a, b, (((ca,), (cb,)), ((), ())), preferred_element_type=f32)


def fused_kernel(
    doc, row_block, slot_of, q, k, v, g, att_o, dq_o, fin_k, fin_v,
    kbuf, vbuf, q_in, g_in, kwin, vwin, qh, gh, qs, gs, s_scr, w_scr, dk_rel, dv_rel,
    out_core, in_core, held, in_one, held_two, in_two, held_z,
    own_sem, tp_send, tp_recv, wide_send, wide_recv, one_send, one_recv, two_send, two_recv,
    core_send, core_recv, res_send, res_recv, r0_send, r0_recv, r1_send, r1_recv,
    r2_send, r2_recv, r3_send, r3_recv,
):
    zh, x, y, core, t = place()
    c = lax.axis_index("ctx")
    enter(c, t, zh, x, y, core)
    peers = near(zh, x, y, core, t)
    sibling = (ctx_of(zh, x, y, 1 - core), t)
    sends = []

    def go(copy):
        copy.start()
        sends.append(copy)
        return copy

    def x_peer(d):
        return (ctx_of(zh, (x + d) % X, y, core), t)

    def y_peer(d):
        return (ctx_of(zh, x, (y + d) % Y, core), t)

    bufs, fins = (kbuf, vbuf), (fin_k, fin_v)

    mine = pl.ds(pl.multiple_of((t % 2) * MINE, MINE), MINE)
    small = {}
    local = {}
    for i, ref in enumerate((k, v)):
        to = bufs[i].at[zh, x, y, core, t // 2, mine, :]
        for n, peer in enumerate(peers):
            small[i, n] = go(remote(
                ref.at[:, columns(peer[1], HEAD)], to, tp_send.at[i, n], tp_recv.at[i, n], peer
            ))
        local[i] = pltpu.make_async_copy(ref.at[:, columns(t, HEAD)], to, own_sem.at[i])
        local[i].start()
    for i, (ref, to) in enumerate(((q, q_in), (g, g_in))):
        local[2 + i] = pltpu.make_async_copy(
            ref.at[:, columns(t, WIDE)], to.at[rows_of(t, MINE), :], own_sem.at[2 + i]
        )
        local[2 + i].start()

    def one_peer(f, d):
        return x_peer(d) if f == 0 else y_peer(d)

    firsts, seconds, siblings, wide = {}, {}, {}, {}

    def spread(i, f, d):
        dx, dy = (-d, 0) if f == 0 else (0, -d)
        here = bufs[i].at[:, (x + dx) % X, (y + dy) % Y, core, f]
        for e in (2, 1, 3):
            seconds[i, f, d, e] = go(remote(
                here, here, two_send.at[i, f, d, e - 1], two_recv.at[i, f, d, e - 1],
                one_peer(1 - f, e),
            ))

    def to_sibling(i, f, e):
        for d in range(4):
            if e > 0:
                seconds[i, f, d, e].wait_recv()
        if f == 0:
            here = bufs[i].at[:, :, (y - e) % Y, core, f]
        else:
            here = bufs[i].at[:, (x - e) % X, :, core, f]
        siblings[i, f, e] = go(remote(
            here, here, core_send.at[i, f, e], core_recv.at[i, f, e], sibling
        ))

    for i in range(2):
        for n in range(len(peers)):
            small[i, n].wait_recv()
        local[i].wait()
        for d in (2, 1, 3):
            for f in range(2):
                here = bufs[i].at[:, x, y, core, f]
                firsts[i, f, d] = go(remote(
                    here, here, one_send.at[i, f, d - 1], one_recv.at[i, f, d - 1], one_peer(f, d)
                ))
        for f in range(2):
            spread(i, f, 0)
    for i, (ref, to) in enumerate(((q, q_in), (g, g_in))):
        for d in (2, 1, 3):
            peer = (t + d) % TP
            wide[i, d] = go(remote(
                ref.at[:, columns(peer, WIDE)], to.at[rows_of(t, MINE), :],
                wide_send.at[i, d - 1], wide_recv.at[i, d - 1], (c, peer),
            ))
    for i in range(2):
        for d in (1, 3, 2):
            for f in range(2):
                firsts[i, f, d].wait_recv()
                spread(i, f, d)
    for f in range(2):
        to_sibling(0, f, 0)
    for e in (1, 3, 2):
        for f in range(2):
            to_sibling(0, f, e)
    for f in range(2):
        to_sibling(1, f, 0)

    def by_head(i, ref, to):
        for d in (1, 2, 3):
            wide[i, d].wait_recv()
        local[2 + i].wait()
        for b in range(2):
            here = pl.ds(b * BLOCK, BLOCK)
            for h in range(GROUP):
                to[b, pl.ds(h * BLOCK, BLOCK), :] = ref[here, pl.ds(h * HEAD, HEAD)]

    by_head(0, q_in, qh)

    offset = lax.broadcasted_iota(jnp.int32, (1, LANES), 1) % BLOCK
    base, low = [], []
    for b in range(2):
        block = row_block[2 * c + b]
        position = block * BLOCK + offset
        lowest = jnp.zeros((1, LANES), jnp.int32)
        end = jnp.int32(0)
        for d in range(DOCS):
            end = end + doc[d]
            lowest = jnp.where(position >= end, end, lowest)
        base.append(block - BACK)
        low.append(lowest - (block - BACK) * BLOCK)

    def in_order(i, to):
        for f in range(2):
            for e in range(4):
                siblings[i, f, e].wait_recv()

        def window(j, carry):
            rows = pl.ds(pl.multiple_of(j * BLOCK, BLOCK), BLOCK)
            for b in range(2):
                s = slot_of[jnp.maximum(base[b] + j, 0)]
                at = tuple(
                    lax.rem(lax.div(s, n), m) for n, m in ((64, 2), (16, 4), (4, 4), (2, 2), (1, 2))
                )
                to[b, rows, :] = bufs[i][at]
            return carry

        lax.fori_loop(0, BACK + 1, window, 0)

    in_order(0, kwin)

    def keys_of(tile):
        return pl.ds(pl.multiple_of(tile * TILE, TILE), TILE)

    tail = pl.ds(BACK * BLOCK, BLOCK)
    at_tile = lax.broadcasted_iota(jnp.int32, (TILE, LANES), 0)
    at_tail = lax.broadcasted_iota(jnp.int32, (BLOCK, LANES), 0)

    def folded(values, fold):
        return fold(values.reshape(values.shape[0] // 8, 8, LANES), axis=0)

    def scores(tile, tops):
        out = []
        for b in range(2):
            s = mm(kwin[b, keys_of(tile), :], qh[b], 1, 1)
            s = jnp.where(at_tile >= low[b] - tile * TILE, s, NEGATIVE)
            s_scr[b, keys_of(tile), :] = s
            out.append(jnp.maximum(tops[b], folded(s, jnp.max)))
        return tuple(out)

    tops = []
    for b in range(2):
        s = mm(kwin[b, tail, :], qh[b], 1, 1)
        seen = (at_tail >= low[b] - BACK * BLOCK) & (at_tail <= offset)
        s = jnp.where(seen, s, NEGATIVE)
        s_scr[b, tail, :] = s
        tops.append(folded(s, jnp.max))
    tops = lax.fori_loop(0, TILES, scores, tuple(tops), unroll=TILES)
    tops = [jnp.max(top, axis=0, keepdims=True) for top in tops]

    for e in (1, 3, 2):
        for f in range(2):
            to_sibling(1, f, e)
    by_head(1, g_in, gh)
    in_order(1, vwin)

    def weigh_part(b, part, total, acc):
        w = jnp.exp2((s_scr[b, part, :] - tops[b]) * SCALE2)
        total = total + folded(w, jnp.sum)
        w16 = w.astype(bf16)
        w_scr[b, part, :] = w16
        return total, acc + mm(vwin[b, part, :], w16, 0, 0)

    def weigh(tile, state):
        out = [weigh_part(b, keys_of(tile), *state[b]) for b in range(2)]
        return tuple(out)

    state = tuple(
        weigh_part(b, tail, jnp.zeros((8, LANES), f32), jnp.zeros((HEAD, LANES), f32))
        for b in range(2)
    )
    state = lax.fori_loop(0, TILES, weigh, state, unroll=TILES)

    inverse, delta = [], []
    results = []

    for b in range(2):
        total, acc = state[b]
        inv = 1.0 / jnp.sum(total, axis=0, keepdims=True)
        att_t = acc * inv
        g_t = gh[b].astype(f32).T
        delta.append(jnp.sum(g_t * att_t, axis=0, keepdims=True))
        inverse.append(inv)
        att = att_t.T.astype(bf16)
        inv_rows = jnp.broadcast_to(inv, (HEAD, LANES)).T
        gs[b] = (gh[b].astype(f32) * inv_rows).astype(bf16)
        qs[b] = (qh[b].astype(f32) * (inv_rows * SCALE)).astype(bf16)
        for h in range(GROUP):
            q_in[pl.ds(b * BLOCK, BLOCK), pl.ds(h * HEAD, HEAD)] = att[h * BLOCK : (h + 1) * BLOCK]

    def send_rows(i, ref, out):
        for d in (2, 1, 3):
            peer = (t + d) % TP
            results.append(go(remote(
                ref.at[rows_of(peer, MINE), :], out.at[:, columns(t, WIDE)],
                res_send.at[i, d - 1], res_recv.at[i, d - 1], (c, peer),
            )))
        local[4 + i] = pltpu.make_async_copy(
            ref.at[rows_of(t, MINE), :], out.at[:, columns(t, WIDE)], own_sem.at[4 + i]
        )
        local[4 + i].start()

    send_rows(0, q_in, att_o)

    def value_part(b, part, first):
        dv = mm(w_scr[b, part, :], gs[b], 1, 0)
        dv_rel[b, pl.ds(first + 1, dv.shape[0] // BLOCK)] = dv.reshape(-1, BLOCK, HEAD)

    def value_tile(tile, carry):
        for b in range(2):
            value_part(b, keys_of(tile), tile * (TILE // BLOCK))
        return carry

    for b in range(2):
        value_part(b, tail, BACK)
    lax.fori_loop(0, TILES, value_tile, 0, unroll=TILES)

    rels = (dk_rel, dv_rel)
    for ref in rels:
        for b in range(2):
            for zero in (0, BACK + 2):
                ref[b, zero] = jnp.zeros((BLOCK, HEAD), f32)

    def piece(i, f, d, e, a, which):
        dx, dy = (d, e) if f == 0 else (e, d)
        s = ctx_of(a, (x + dx) % X, (y + dy) % Y, which) * 2 + f
        total = None
        for b in range(2):
            rel = row_block[s] - base[b] + 1
            part = rels[i][b, jnp.minimum(jnp.maximum(rel, 0), BACK + 2)]
            total = part if total is None else total + part
        return total

    order = [(d, f) for d in (2, 1, 3, 0) for f in range(2)]
    r0 = {}

    def assemble(i):
        for d, f in order:
            def fill(e, carry):
                for a in range(ZH):
                    out_core[i, f, d, e, a] = piece(i, f, d, e, a, 1 - core).astype(bf16)
                return carry

            lax.fori_loop(0, 4, fill, 0)
            r0[i, f, d] = go(remote(
                out_core.at[i, f, d], in_core.at[i, f, d],
                r0_send.at[i, f, d], r0_recv.at[i, f, d], sibling,
            ))

    def r1(i, f, d, e):
        return remote(
            held.at[i, f, d, e], in_one.at[i, f, d - 1, e], r1_send.at[i, f, d - 1, e],
            r1_recv.at[i, f, d - 1, e], one_peer(f, d),
        )

    def join(i):
        for d, f in order:
            r0[i, f, d].wait_recv()

            def add(n, carry):
                e = (n + 1) % 4
                for a in range(ZH):
                    total = piece(i, f, d, e, a, core) + in_core[i, f, d, e, a].astype(f32)
                    held[i, f, d, e, a] = total.astype(bf16)
                if d > 0:
                    r1(i, f, d, e).start()
                return carry

            lax.fori_loop(0, 4, add, 0)

    def back_part(b, part, first, dq_t):
        keys = kwin[b, part, :]
        dp = mm(vwin[b, part, :], gh[b], 1, 1)
        ds = (w_scr[b, part, :].astype(f32) * (dp - delta[b])).astype(bf16)
        dk = mm(ds, qs[b], 1, 0)
        dk_rel[b, pl.ds(first + 1, dk.shape[0] // BLOCK)] = dk.reshape(-1, BLOCK, HEAD)
        return dq_t + mm(keys, ds, 0, 0)

    def back(b):
        def step(tile, dq_t):
            return back_part(b, keys_of(tile), tile * (TILE // BLOCK), dq_t)

        dq_t = back_part(b, tail, BACK, jnp.zeros((HEAD, LANES), f32))
        dq_t = lax.fori_loop(0, TILES, step, dq_t, unroll=TILES)
        dq = (dq_t * (inverse[b] * SCALE)).T.astype(bf16)
        for h in range(GROUP):
            g_in[pl.ds(b * BLOCK, BLOCK), pl.ds(h * HEAD, HEAD)] = dq[h * BLOCK : (h + 1) * BLOCK]

    assemble(1)
    join(1)
    back(0)
    back(1)
    assemble(0)
    send_rows(1, g_in, dq_o)
    join(0)

    def r2(i, f, e):
        return remote(
            held_two.at[i, f, e], in_two.at[i, f, e - 1], r2_send.at[i, f, e - 1],
            r2_recv.at[i, f, e - 1], one_peer(1 - f, e),
        )

    for i in (1, 0):
        for e in (1, 2, 3, 0):
            for f in range(2):
                for d in (1, 3, 2):
                    r1(i, f, d, e).wait_recv()
                for a in range(ZH):
                    total = held[i, f, 0, e, a].astype(f32)
                    for d in range(3):
                        total = total + in_one[i, f, d, e, a].astype(f32)
                    held_two[i, f, e, a] = total.astype(bf16)
                if e > 0:
                    go(r2(i, f, e))

    last = {}
    for i in (1, 0):
        for f in range(2):
            for e in (1, 2, 3):
                r2(i, f, e).wait_recv()
            for a in range(ZH):
                total = held_two[i, f, 0, a].astype(f32)
                for e in range(3):
                    total = total + in_two[i, f, e, a].astype(f32)
                held_z[i, a, f] = total.astype(bf16)
        for n, peer in enumerate(peers):
            a = (zh + (n + 1) // TP) % ZH
            last[i, n] = go(remote(
                held_z.at[i, a, peer[1] // 2, pl.ds(pl.multiple_of((peer[1] % 2) * MINE, MINE), MINE), :],
                fins[i].at[zh, t], r3_send.at[i, n], r3_recv.at[i, n], peer,
            ))
        local[6 + i] = pltpu.make_async_copy(
            held_z.at[i, zh, t // 2, mine, :], fins[i].at[zh, t], own_sem.at[6 + i]
        )
        local[6 + i].start()
    for copy in last.values():
        copy.wait_recv()
    for copy in results:
        copy.wait_recv()
    for i in range(4, 8):
        local[i].wait()
    for copy in sends:
        copy.wait_send()
    for i in range(2):
        for f in range(2):
            for d in range(1, 4):
                for e in range(4):
                    r1(i, f, d, e).wait_send()


def fused(doc_lengths, row_block, queries, keys, values, out_grad):
    dma = pltpu.SemaphoreType.DMA
    anywhere = pl.BlockSpec(memory_space=pl.ANY)
    smem = pl.BlockSpec(memory_space=pltpu.SMEM)
    V = pltpu.VMEM
    slots = (ZH, X, Y, CORE, 2, BLOCK, HEAD)
    piece = (BLOCK, HEAD)
    number = jnp.arange(NBLK, dtype=jnp.int32)
    found = row_block[None, :] == number[:, None]
    slot_of = jnp.sum(jnp.where(found, number[None, :], 0), axis=1)
    return pl.pallas_call(
        fused_kernel,
        out_shape=(
            jax.ShapeDtypeStruct((MINE, TP * WIDE), bf16),
            jax.ShapeDtypeStruct((MINE, TP * WIDE), bf16),
            jax.ShapeDtypeStruct((ZH, TP, MINE, HEAD), bf16),
            jax.ShapeDtypeStruct((ZH, TP, MINE, HEAD), bf16),
        ),
        in_specs=[smem, smem, smem] + [anywhere] * 4,
        out_specs=[anywhere] * 4,
        scratch_shapes=[
            V(slots, bf16), V(slots, bf16),
            V((ROWS, WIDE), bf16), V((ROWS, WIDE), bf16),
            V((2, WINDOW, HEAD), bf16), V((2, WINDOW, HEAD), bf16),
            V((2, LANES, HEAD), bf16), V((2, LANES, HEAD), bf16),
            V((2, LANES, HEAD), bf16), V((2, LANES, HEAD), bf16),
            V((2, WINDOW, LANES), f32), V((2, WINDOW, LANES), bf16),
            V((2, BACK + 3, BLOCK, HEAD), f32), V((2, BACK + 3, BLOCK, HEAD), f32),
            V((2, 2, 4, 4, ZH) + piece, bf16), V((2, 2, 4, 4, ZH) + piece, bf16),
            V((2, 2, 4, 4, ZH) + piece, bf16), V((2, 2, 3, 4, ZH) + piece, bf16),
            V((2, 2, 4, ZH) + piece, bf16), V((2, 2, 3, ZH) + piece, bf16),
            V((2, ZH, 2) + piece, bf16),
            dma((8,)),
            dma((2, 7)), dma((2, 7)),
            dma((2, 3)), dma((2, 3)),
            dma((2, 2, 3)), dma((2, 2, 3)),
            dma((2, 2, 4, 3)), dma((2, 2, 4, 3)),
            dma((2, 2, 4)), dma((2, 2, 4)),
            dma((2, 3)), dma((2, 3)),
            dma((2, 2, 4)), dma((2, 2, 4)),
            dma((2, 2, 3, 4)), dma((2, 2, 3, 4)),
            dma((2, 2, 3)), dma((2, 2, 3)),
            dma((2, 7)), dma((2, 7)),
        ],
        compiler_params=pltpu.CompilerParams(
            collective_id=0, has_side_effects=True, vmem_limit_bytes=VMEM_LIMIT
        ),
        name="fused",
    )(doc_lengths, row_block, slot_of, queries, keys, values, out_grad)


def hand_over_kernel(*refs):
    held, sums, sems = refs[8:12], refs[12:14], refs[14]
    arrive = [pltpu.make_async_copy(refs[i], held[i], sems.at[0, i]) for i in range(4)]
    from_where = held[:2] + sums
    leave = [pltpu.make_async_copy(from_where[i], refs[4 + i], sems.at[1, i]) for i in range(4)]
    for copy in arrive:
        copy.start()
    for i in range(4):
        arrive[i].wait()
        if i >= 2:
            for h in range(TP):
                total = held[i][0, h].astype(f32) + held[i][1, h].astype(f32)
                sums[i - 2][:, pl.ds(h * HEAD, HEAD)] = total.astype(bf16)
        leave[i].start()
    for copy in leave:
        copy.wait()


def hand_over(arrays):
    anywhere = pl.BlockSpec(memory_space=pl.ANY)
    narrow = jax.ShapeDtypeStruct((MINE, TP * HEAD), bf16)
    return pl.pallas_call(
        hand_over_kernel,
        out_shape=tuple(jax.ShapeDtypeStruct(a.shape, a.dtype) for a in arrays[:2]) + (narrow,) * 2,
        in_specs=[anywhere] * 4,
        out_specs=[anywhere] * 4,
        scratch_shapes=[pltpu.VMEM(a.shape, a.dtype) for a in arrays]
        + [pltpu.VMEM(narrow.shape, bf16)] * 2
        + [pltpu.SemaphoreType.DMA((2, 4))],
        name="hand_over",
    )(*arrays)


def per_device(queries, keys, values, out_grad, doc_lengths, row_block):
    return hand_over(fused(doc_lengths, row_block, queries, keys, values, out_grad))


def solution(mesh):
    return jax.shard_map(
        per_device,
        mesh=mesh,
        in_specs=(P(("ctx", "tp"), None),) * 4 + (P(), P()),
        out_specs=(P(("ctx", "tp"), None),) * 4,
        check_vma=False,
    )
```

```python
import math

import jax
import jax.numpy as jnp
from jax import lax
from jax.experimental import pallas as pl
from jax.experimental.pallas import tpu as pltpu
from jax.sharding import PartitionSpec as P

HEAD = 128
BLOCK = 64
GROUP = 8
DOCS = 16
NBLK = 128
ZH, X, Y, CORE, TP = 2, 4, 4, 2, 4
ROWS = 2 * BLOCK
MINE = ROWS // TP
WIDE = GROUP * HEAD
TILE = 512
BACK = 2048 // BLOCK
WINDOW = (BACK + 1) * BLOCK
TILES = BACK * BLOCK // TILE
LANES = GROUP * BLOCK
SCALE = 1.0 / math.sqrt(HEAD)
SCALE2 = SCALE * math.log2(math.e)
NEGATIVE = -1e30
VMEM_LIMIT = 56 * 1024 * 1024
f32 = jnp.float32
bf16 = jnp.bfloat16


def place():
    c = lax.axis_index("ctx")
    t = lax.axis_index("tp")
    return c // 32, (c // 8) % 4, (c // 2) % 4, c % 2, t


def ctx_of(zh, x, y, core):
    return ((zh * X + x) * Y + y) * CORE + core


def enter(me, t, zh, x, y, core):
    barrier = pltpu.get_barrier_semaphore()
    peers = near(zh, x, y, core, t)
    peers += [(ctx_of(zh, (x + d) % X, y, core), t) for d in range(1, X)]
    peers += [(ctx_of(zh, x, (y + d) % Y, core), t) for d in range(1, Y)]
    peers += [(ctx_of(zh, x, y, 1 - core), t)]
    for peer in peers:
        pl.semaphore_signal(barrier, inc=1, device_id=peer, device_id_type=pl.DeviceIdType.MESH)
    pl.semaphore_wait(barrier, len(peers))


def near(zh, x, y, core, t):
    return [
        (ctx_of((zh + a) % ZH, x, y, core), (t + d) % TP)
        for a in range(ZH)
        for d in range(TP)
        if a + d > 0
    ]


def remote(src, dst, send, recv, peer):
    return pltpu.make_async_remote_copy(
        src_ref=src,
        dst_ref=dst,
        send_sem=send,
        recv_sem=recv,
        device_id=peer,
        device_id_type=pl.DeviceIdType.MESH,
    )


def columns(index, width):
    return pl.ds(pl.multiple_of(index * width, width), width)


def rows_of(index, count):
    return pl.ds(pl.multiple_of(index * count, count), count)


def mm(a, b, ca, cb):
    return lax.dot_general(a, b, (((ca,), (cb,)), ((), ())), preferred_element_type=f32)


def fused_kernel(
    doc, row_block, slot_of, q, k, v, g, att_o, dq_o, fin_k, fin_v,
    kbuf, vbuf, q_in, g_in, kwin, vwin, qh, gh, qs, gs, s_scr, w_scr, dk_rel, dv_rel,
    out_core, in_core, held, in_one, held_two, in_two, held_z,
    own_sem, tp_send, tp_recv, wide_send, wide_recv, one_send, one_recv, two_send, two_recv,
    core_send, core_recv, res_send, res_recv, r0_send, r0_recv, r1_send, r1_recv,
    r2_send, r2_recv, r3_send, r3_recv,
):
    zh, x, y, core, t = place()
    c = lax.axis_index("ctx")
    enter(c, t, zh, x, y, core)
    peers = near(zh, x, y, core, t)
    sibling = (ctx_of(zh, x, y, 1 - core), t)
    sends = []

    def go(copy):
        copy.start()
        sends.append(copy)
        return copy

    def x_peer(d):
        return (ctx_of(zh, (x + d) % X, y, core), t)

    def y_peer(d):
        return (ctx_of(zh, x, (y + d) % Y, core), t)

    bufs, fins = (kbuf, vbuf), (fin_k, fin_v)

    mine = pl.ds(pl.multiple_of((t % 2) * MINE, MINE), MINE)
    small = {}
    local = {}
    for i, ref in enumerate((k, v)):
        to = bufs[i].at[zh, x, y, core, t // 2, mine, :]
        for n, peer in enumerate(peers):
            small[i, n] = go(remote(
                ref.at[:, columns(peer[1], HEAD)], to, tp_send.at[i, n], tp_recv.at[i, n], peer
            ))
        local[i] = pltpu.make_async_copy(ref.at[:, columns(t, HEAD)], to, own_sem.at[i])
        local[i].start()
    for i, (ref, to) in enumerate(((q, q_in), (g, g_in))):
        local[2 + i] = pltpu.make_async_copy(
            ref.at[:, columns(t, WIDE)], to.at[rows_of(t, MINE), :], own_sem.at[2 + i]
        )
        local[2 + i].start()

    def one_peer(f, d):
        return x_peer(d) if f == 0 else y_peer(d)

    firsts, seconds, siblings, wide = {}, {}, {}, {}

    def spread(i, f, d):
        dx, dy = (-d, 0) if f == 0 else (0, -d)
        here = bufs[i].at[:, (x + dx) % X, (y + dy) % Y, core, f]
        for e in (1, 3):
            seconds[i, f, d, e] = go(remote(
                here, here, two_send.at[i, f, d, e], two_recv.at[i, f, d, e], one_peer(1 - f, e)
            ))

    def relay(i, f, d):
        for a, e in ((0, 1), (1, 3)):
            seconds[i, f, d, e].wait_recv()
            dx, dy = (-d, -e) if f == 0 else (-e, -d)
            here = bufs[i].at[a, (x + dx) % X, (y + dy) % Y, core, f]
            seconds[i, f, d, 2 * a] = go(remote(
                here, here, two_send.at[i, f, d, 2 * a], two_recv.at[i, f, d, 2 * a],
                one_peer(1 - f, e),
            ))

    def to_sibling(i, f, e):
        for d in range(4):
            if e == 2:
                seconds[i, f, d, 0].wait_recv()
                seconds[i, f, d, 2].wait_recv()
        if f == 0:
            here = bufs[i].at[:, :, (y - e) % Y, core, f]
        else:
            here = bufs[i].at[:, (x - e) % X, :, core, f]
        siblings[i, f, e] = go(remote(
            here, here, core_send.at[i, f, e], core_recv.at[i, f, e], sibling
        ))

    def begin(i):
        for n in range(len(peers)):
            small[i, n].wait_recv()
        local[i].wait()
        for d in (2, 1, 3):
            for f in range(2):
                here = bufs[i].at[:, x, y, core, f]
                firsts[i, f, d] = go(remote(
                    here, here, one_send.at[i, f, d - 1], one_recv.at[i, f, d - 1], one_peer(f, d)
                ))
        for f in range(2):
            spread(i, f, 0)

    def go_on(i, d):
        for f in range(2):
            firsts[i, f, d].wait_recv()
            spread(i, f, d)

    begin(0)
    for i, (ref, to) in enumerate(((q, q_in), (g, g_in))):
        for d in (2, 1, 3):
            peer = (t + d) % TP
            wide[i, d] = go(remote(
                ref.at[:, columns(peer, WIDE)], to.at[rows_of(t, MINE), :],
                wide_send.at[i, d - 1], wide_recv.at[i, d - 1], (c, peer),
            ))
    begin(1)
    for i in range(2):
        for d in (1, 3, 2):
            go_on(i, d)
    for i in range(2):
        for d in (0, 1, 3, 2):
            for f in range(2):
                relay(i, f, d)
        for e in (0, 1, 3):
            for f in range(2):
                to_sibling(i, f, e)
    for f in range(2):
        to_sibling(0, f, 2)

    def by_head(i, ref, to):
        for d in (1, 2, 3):
            wide[i, d].wait_recv()
        local[2 + i].wait()
        for b in range(2):
            here = pl.ds(b * BLOCK, BLOCK)
            for h in range(GROUP):
                to[b, pl.ds(h * BLOCK, BLOCK), :] = ref[here, pl.ds(h * HEAD, HEAD)]

    by_head(0, q_in, qh)

    offset = lax.broadcasted_iota(jnp.int32, (1, LANES), 1) % BLOCK
    base, low = [], []
    for b in range(2):
        block = row_block[2 * c + b]
        position = block * BLOCK + offset
        lowest = jnp.zeros((1, LANES), jnp.int32)
        end = jnp.int32(0)
        for d in range(DOCS):
            end = end + doc[d]
            lowest = jnp.where(position >= end, end, lowest)
        base.append(block - BACK)
        low.append(lowest - (block - BACK) * BLOCK)

    def in_order(i, to):
        for f in range(2):
            for e in range(4):
                siblings[i, f, e].wait_recv()

        def window(j, carry):
            rows = pl.ds(pl.multiple_of(j * BLOCK, BLOCK), BLOCK)
            for b in range(2):
                s = slot_of[jnp.maximum(base[b] + j, 0)]
                at = tuple(
                    lax.rem(lax.div(s, n), m) for n, m in ((64, 2), (16, 4), (4, 4), (2, 2), (1, 2))
                )
                to[b, rows, :] = bufs[i][at]
            return carry

        lax.fori_loop(0, BACK + 1, window, 0, unroll=11)

    in_order(0, kwin)

    def keys_of(tile):
        return pl.ds(pl.multiple_of(tile * TILE, TILE), TILE)

    tail = pl.ds(BACK * BLOCK, BLOCK)
    at_tile = lax.broadcasted_iota(jnp.int32, (TILE, LANES), 0)
    at_tail = lax.broadcasted_iota(jnp.int32, (BLOCK, LANES), 0)

    def folded(values, fold):
        return fold(values.reshape(values.shape[0] // 8, 8, LANES), axis=0)

    def scores(tile, tops):
        out = []
        for b in range(2):
            s = mm(kwin[b, keys_of(tile), :], qh[b], 1, 1)
            s = jnp.where(at_tile >= low[b] - tile * TILE, s, NEGATIVE)
            s_scr[b, keys_of(tile), :] = s
            out.append(jnp.maximum(tops[b], folded(s, jnp.max)))
        return tuple(out)

    tops = []
    for b in range(2):
        s = mm(kwin[b, tail, :], qh[b], 1, 1)
        seen = (at_tail >= low[b] - BACK * BLOCK) & (at_tail <= offset)
        s = jnp.where(seen, s, NEGATIVE)
        s_scr[b, tail, :] = s
        tops.append(folded(s, jnp.max))
    tops = lax.fori_loop(0, TILES, scores, tuple(tops), unroll=TILES)
    tops = [jnp.max(top, axis=0, keepdims=True) for top in tops]

    for f in range(2):
        to_sibling(1, f, 2)
    by_head(1, g_in, gh)
    in_order(1, vwin)

    def weigh_part(b, part, total, acc):
        w = jnp.exp2((s_scr[b, part, :] - tops[b]) * SCALE2)
        total = total + folded(w, jnp.sum)
        w16 = w.astype(bf16)
        w_scr[b, part, :] = w16
        return total, acc + mm(vwin[b, part, :], w16, 0, 0)

    def weigh(tile, state):
        out = [weigh_part(b, keys_of(tile), *state[b]) for b in range(2)]
        return tuple(out)

    state = tuple(
        weigh_part(b, tail, jnp.zeros((8, LANES), f32), jnp.zeros((HEAD, LANES), f32))
        for b in range(2)
    )
    state = lax.fori_loop(0, TILES, weigh, state, unroll=TILES)

    inverse, inv_rows, delta = [], [], []
    for b in range(2):
        inv = 1.0 / jnp.sum(state[b][0], axis=0, keepdims=True)
        inverse.append(inv)
        inv_rows.append(jnp.broadcast_to(inv, (HEAD, LANES)).T)
        gs[b] = (gh[b].astype(f32) * inv_rows[b]).astype(bf16)

    results = []

    def send_rows(i, ref, out):
        for d in (2, 1, 3):
            peer = (t + d) % TP
            results.append(go(remote(
                ref.at[rows_of(peer, MINE), :], out.at[:, columns(t, WIDE)],
                res_send.at[i, d - 1], res_recv.at[i, d - 1], (c, peer),
            )))
        local[4 + i] = pltpu.make_async_copy(
            ref.at[rows_of(t, MINE), :], out.at[:, columns(t, WIDE)], own_sem.at[4 + i]
        )
        local[4 + i].start()

    def value_part(b, part, first):
        dv = mm(w_scr[b, part, :], gs[b], 1, 0)
        dv_rel[b, pl.ds(first + 1, dv.shape[0] // BLOCK)] = dv.reshape(-1, BLOCK, HEAD)

    def value_tile(tile, carry):
        for b in range(2):
            value_part(b, keys_of(tile), tile * (TILE // BLOCK))
        return carry

    for b in range(2):
        value_part(b, tail, BACK)
    lax.fori_loop(0, TILES, value_tile, 0, unroll=TILES)

    rels = (dk_rel, dv_rel)
    for ref in rels:
        for b in range(2):
            for zero in (0, BACK + 2):
                ref[b, zero] = jnp.zeros((BLOCK, HEAD), f32)

    def piece(i, f, d, e, a, which):
        dx, dy = (d, e) if f == 0 else (e, d)
        s = ctx_of(a, (x + dx) % X, (y + dy) % Y, which) * 2 + f
        total = None
        for b in range(2):
            rel = row_block[s] - base[b] + 1
            part = rels[i][b, jnp.minimum(jnp.maximum(rel, 0), BACK + 2)]
            total = part if total is None else total + part
        return total

    order = [(d, f) for d in (2, 1, 3, 0) for f in range(2)]
    r0 = {}

    def assemble(i):
        for d, f in order:
            def fill(e, carry):
                for a in range(ZH):
                    out_core[i, f, d, e, a] = piece(i, f, d, e, a, 1 - core).astype(bf16)
                return carry

            lax.fori_loop(0, 4, fill, 0, unroll=4)
            r0[i, f, d] = go(remote(
                out_core.at[i, f, d], in_core.at[i, f, d],
                r0_send.at[i, f, d], r0_recv.at[i, f, d], sibling,
            ))

    def r1(i, f, d, e):
        return remote(
            held.at[i, f, d, e], in_one.at[i, f, d - 1, e], r1_send.at[i, f, d - 1, e],
            r1_recv.at[i, f, d - 1, e], one_peer(f, d),
        )

    def join(i):
        for d, f in order:
            r0[i, f, d].wait_recv()

            def add(n, carry):
                e = (n + 1) % 4
                for a in range(ZH):
                    total = piece(i, f, d, e, a, core) + in_core[i, f, d, e, a].astype(f32)
                    held[i, f, d, e, a] = total.astype(bf16)
                if d > 0:
                    r1(i, f, d, e).start()
                return carry

            lax.fori_loop(0, 4, add, 0, unroll=4)

    def back_part(b, part, first, dq_t):
        keys = kwin[b, part, :]
        dp = mm(vwin[b, part, :], gh[b], 1, 1)
        ds = (w_scr[b, part, :].astype(f32) * (dp - delta[b])).astype(bf16)
        dk = mm(ds, qs[b], 1, 0)
        dk_rel[b, pl.ds(first + 1, dk.shape[0] // BLOCK)] = dk.reshape(-1, BLOCK, HEAD)
        return dq_t + mm(keys, ds, 0, 0)

    def back(b):
        def step(tile, dq_t):
            return back_part(b, keys_of(tile), tile * (TILE // BLOCK), dq_t)

        dq_t = back_part(b, tail, BACK, jnp.zeros((HEAD, LANES), f32))
        dq_t = lax.fori_loop(0, TILES, step, dq_t, unroll=TILES)
        dq = (dq_t * (inverse[b] * SCALE)).T.astype(bf16)
        for h in range(GROUP):
            g_in[pl.ds(b * BLOCK, BLOCK), pl.ds(h * HEAD, HEAD)] = dq[h * BLOCK : (h + 1) * BLOCK]

    assemble(1)
    for b in range(2):
        att_t = state[b][1] * inverse[b]
        delta.append(jnp.sum(gh[b].astype(f32).T * att_t, axis=0, keepdims=True))
        att = att_t.T.astype(bf16)
        qs[b] = (qh[b].astype(f32) * (inv_rows[b] * SCALE)).astype(bf16)
        for h in range(GROUP):
            q_in[pl.ds(b * BLOCK, BLOCK), pl.ds(h * HEAD, HEAD)] = att[h * BLOCK : (h + 1) * BLOCK]
    send_rows(0, q_in, att_o)
    join(1)
    back(0)
    back(1)
    assemble(0)
    send_rows(1, g_in, dq_o)
    join(0)

    def r2(i, f, e):
        return remote(
            held_two.at[i, f, e], in_two.at[i, f, e - 1], r2_send.at[i, f, e - 1],
            r2_recv.at[i, f, e - 1], one_peer(1 - f, e),
        )

    for i in (1, 0):
        for e in (1, 2, 3, 0):
            for f in range(2):
                for d in (1, 3, 2):
                    r1(i, f, d, e).wait_recv()
                for a in range(ZH):
                    total = held[i, f, 0, e, a].astype(f32)
                    for d in range(3):
                        total = total + in_one[i, f, d, e, a].astype(f32)
                    held_two[i, f, e, a] = total.astype(bf16)
                if e > 0:
                    go(r2(i, f, e))

    last = {}
    for i in (1, 0):
        for f in range(2):
            for e in (1, 2, 3):
                r2(i, f, e).wait_recv()
            for a in range(ZH):
                total = held_two[i, f, 0, a].astype(f32)
                for e in range(3):
                    total = total + in_two[i, f, e, a].astype(f32)
                held_z[i, a, f] = total.astype(bf16)
        for n, peer in enumerate(peers):
            a = (zh + (n + 1) // TP) % ZH
            last[i, n] = go(remote(
                held_z.at[i, a, peer[1] // 2, pl.ds(pl.multiple_of((peer[1] % 2) * MINE, MINE), MINE), :],
                fins[i].at[zh, t], r3_send.at[i, n], r3_recv.at[i, n], peer,
            ))
        local[6 + i] = pltpu.make_async_copy(
            held_z.at[i, zh, t // 2, mine, :], fins[i].at[zh, t], own_sem.at[6 + i]
        )
        local[6 + i].start()
    for copy in last.values():
        copy.wait_recv()
    for copy in results:
        copy.wait_recv()
    for i in range(4, 8):
        local[i].wait()
    for copy in sends:
        copy.wait_send()
    for i in range(2):
        for f in range(2):
            for d in range(1, 4):
                for e in range(4):
                    r1(i, f, d, e).wait_send()


def fused(doc_lengths, row_block, queries, keys, values, out_grad):
    dma = pltpu.SemaphoreType.DMA
    anywhere = pl.BlockSpec(memory_space=pl.ANY)
    smem = pl.BlockSpec(memory_space=pltpu.SMEM)
    V = pltpu.VMEM
    slots = (ZH, X, Y, CORE, 2, BLOCK, HEAD)
    piece = (BLOCK, HEAD)
    number = jnp.arange(NBLK, dtype=jnp.int32)
    found = row_block[None, :] == number[:, None]
    slot_of = jnp.sum(jnp.where(found, number[None, :], 0), axis=1)
    return pl.pallas_call(
        fused_kernel,
        out_shape=(
            jax.ShapeDtypeStruct((MINE, TP * WIDE), bf16),
            jax.ShapeDtypeStruct((MINE, TP * WIDE), bf16),
            jax.ShapeDtypeStruct((ZH, TP, MINE, HEAD), bf16),
            jax.ShapeDtypeStruct((ZH, TP, MINE, HEAD), bf16),
        ),
        in_specs=[smem, smem, smem] + [anywhere] * 4,
        out_specs=[anywhere] * 4,
        scratch_shapes=[
            V(slots, bf16), V(slots, bf16),
            V((ROWS, WIDE), bf16), V((ROWS, WIDE), bf16),
            V((2, WINDOW, HEAD), bf16), V((2, WINDOW, HEAD), bf16),
            V((2, LANES, HEAD), bf16), V((2, LANES, HEAD), bf16),
            V((2, LANES, HEAD), bf16), V((2, LANES, HEAD), bf16),
            V((2, WINDOW, LANES), f32), V((2, WINDOW, LANES), bf16),
            V((2, BACK + 3, BLOCK, HEAD), f32), V((2, BACK + 3, BLOCK, HEAD), f32),
            V((2, 2, 4, 4, ZH) + piece, bf16), V((2, 2, 4, 4, ZH) + piece, bf16),
            V((2, 2, 4, 4, ZH) + piece, bf16), V((2, 2, 3, 4, ZH) + piece, bf16),
            V((2, 2, 4, ZH) + piece, bf16), V((2, 2, 3, ZH) + piece, bf16),
            V((2, ZH, 2) + piece, bf16),
            dma((8,)),
            dma((2, 7)), dma((2, 7)),
            dma((2, 3)), dma((2, 3)),
            dma((2, 2, 3)), dma((2, 2, 3)),
            dma((2, 2, 4, 4)), dma((2, 2, 4, 4)),
            dma((2, 2, 4)), dma((2, 2, 4)),
            dma((2, 3)), dma((2, 3)),
            dma((2, 2, 4)), dma((2, 2, 4)),
            dma((2, 2, 3, 4)), dma((2, 2, 3, 4)),
            dma((2, 2, 3)), dma((2, 2, 3)),
            dma((2, 7)), dma((2, 7)),
        ],
        compiler_params=pltpu.CompilerParams(
            collective_id=0, has_side_effects=True, vmem_limit_bytes=VMEM_LIMIT
        ),
        name="fused",
    )(doc_lengths, row_block, slot_of, queries, keys, values, out_grad)


def hand_over_kernel(*refs):
    held, sums, sems = refs[8:12], refs[12:14], refs[14]
    arrive = [pltpu.make_async_copy(refs[i], held[i], sems.at[0, i]) for i in range(4)]
    from_where = held[:2] + sums
    leave = [pltpu.make_async_copy(from_where[i], refs[4 + i], sems.at[1, i]) for i in range(4)]
    for copy in arrive:
        copy.start()
    for i in range(4):
        arrive[i].wait()
        if i >= 2:
            for h in range(TP):
                total = held[i][0, h].astype(f32) + held[i][1, h].astype(f32)
                sums[i - 2][:, pl.ds(h * HEAD, HEAD)] = total.astype(bf16)
        leave[i].start()
    for copy in leave:
        copy.wait()


def hand_over(arrays):
    anywhere = pl.BlockSpec(memory_space=pl.ANY)
    narrow = jax.ShapeDtypeStruct((MINE, TP * HEAD), bf16)
    return pl.pallas_call(
        hand_over_kernel,
        out_shape=tuple(jax.ShapeDtypeStruct(a.shape, a.dtype) for a in arrays[:2]) + (narrow,) * 2,
        in_specs=[anywhere] * 4,
        out_specs=[anywhere] * 4,
        scratch_shapes=[pltpu.VMEM(a.shape, a.dtype) for a in arrays]
        + [pltpu.VMEM(narrow.shape, bf16)] * 2
        + [pltpu.SemaphoreType.DMA((2, 4))],
        name="hand_over",
    )(*arrays)


def per_device(queries, keys, values, out_grad, doc_lengths, row_block):
    return hand_over(fused(doc_lengths, row_block, queries, keys, values, out_grad))


def solution(mesh):
    return jax.shard_map(
        per_device,
        mesh=mesh,
        in_specs=(P(("ctx", "tp"), None),) * 4 + (P(), P()),
        out_specs=(P(("ctx", "tp"), None),) * 4,
        check_vma=False,
    )
```

```python
import math

import jax
import jax.numpy as jnp
from jax import lax
from jax.experimental import pallas as pl
from jax.experimental.pallas import tpu as pltpu
from jax.sharding import PartitionSpec as P

HEAD = 128
BLOCK = 64
GROUP = 8
DOCS = 16
NBLK = 128
ZH, X, Y, CORE, TP = 2, 4, 4, 2, 4
ROWS = 2 * BLOCK
MINE = ROWS // TP
WIDE = GROUP * HEAD
TILE = 512
BACK = 2048 // BLOCK
WINDOW = (BACK + 1) * BLOCK
TILES = BACK * BLOCK // TILE
LANES = GROUP * BLOCK
SCALE = 1.0 / math.sqrt(HEAD)
SCALE2 = SCALE * math.log2(math.e)
NEGATIVE = -1e30
VMEM_LIMIT = 56 * 1024 * 1024
f32 = jnp.float32
bf16 = jnp.bfloat16


def place():
    c = lax.axis_index("ctx")
    t = lax.axis_index("tp")
    return c // 32, (c // 8) % 4, (c // 2) % 4, c % 2, t


def ctx_of(zh, x, y, core):
    return ((zh * X + x) * Y + y) * CORE + core


def enter(me, t, zh, x, y, core):
    barrier = pltpu.get_barrier_semaphore()
    peers = near(zh, x, y, core, t)
    peers += [(ctx_of(zh, (x + d) % X, y, core), t) for d in range(1, X)]
    peers += [(ctx_of(zh, x, (y + d) % Y, core), t) for d in range(1, Y)]
    peers += [(ctx_of(zh, x, y, 1 - core), t)]
    for peer in peers:
        pl.semaphore_signal(barrier, inc=1, device_id=peer, device_id_type=pl.DeviceIdType.MESH)
    pl.semaphore_wait(barrier, len(peers))


def near(zh, x, y, core, t):
    return [
        (ctx_of((zh + a) % ZH, x, y, core), (t + d) % TP)
        for a in range(ZH)
        for d in range(TP)
        if a + d > 0
    ]


def remote(src, dst, send, recv, peer):
    return pltpu.make_async_remote_copy(
        src_ref=src,
        dst_ref=dst,
        send_sem=send,
        recv_sem=recv,
        device_id=peer,
        device_id_type=pl.DeviceIdType.MESH,
    )


def columns(index, width):
    return pl.ds(pl.multiple_of(index * width, width), width)


def rows_of(index, count):
    return pl.ds(pl.multiple_of(index * count, count), count)


def mm(a, b, ca, cb):
    return lax.dot_general(a, b, (((ca,), (cb,)), ((), ())), preferred_element_type=f32)


def fused_kernel(
    doc, row_block, row_vector, q, k, v, g, att_o, dq_o, fin_k, fin_v,
    kbuf, vbuf, q_in, g_in, kwin, vwin, qh, gh, qs, gs, s_scr, w_scr, dk_rel, dv_rel,
    slot_v, slot_of, out_core, in_core, held, in_one, held_two, in_two, held_z,
    own_sem, tp_send, tp_recv, wide_send, wide_recv, one_send, one_recv, two_send, two_recv,
    core_send, core_recv, res_send, res_recv, r0_send, r0_recv, r1_send, r1_recv,
    r2_send, r2_recv, r3_send, r3_recv,
):
    zh, x, y, core, t = place()
    c = lax.axis_index("ctx")
    enter(c, t, zh, x, y, core)
    peers = near(zh, x, y, core, t)
    sibling = (ctx_of(zh, x, y, 1 - core), t)
    sends = []

    def go(copy):
        copy.start()
        sends.append(copy)
        return copy

    def x_peer(d):
        return (ctx_of(zh, (x + d) % X, y, core), t)

    def y_peer(d):
        return (ctx_of(zh, x, (y + d) % Y, core), t)

    bufs, fins = (kbuf, vbuf), (fin_k, fin_v)

    mine = pl.ds(pl.multiple_of((t % 2) * MINE, MINE), MINE)
    small = {}
    local = {}
    for i, ref in enumerate((k, v)):
        to = bufs[i].at[zh, x, y, core, t // 2, mine, :]
        for n, peer in enumerate(peers):
            small[i, n] = go(remote(
                ref.at[:, columns(peer[1], HEAD)], to, tp_send.at[i, n], tp_recv.at[i, n], peer
            ))
        local[i] = pltpu.make_async_copy(ref.at[:, columns(t, HEAD)], to, own_sem.at[i])
        local[i].start()
    for i, (ref, to) in enumerate(((q, q_in), (g, g_in))):
        local[2 + i] = pltpu.make_async_copy(
            ref.at[:, columns(t, WIDE)], to.at[rows_of(t, MINE), :], own_sem.at[2 + i]
        )
        local[2 + i].start()

    held_blocks = jnp.broadcast_to(row_vector[...], (NBLK, NBLK)).T
    wanted = lax.broadcasted_iota(jnp.int32, (NBLK, NBLK), 1)
    number = lax.broadcasted_iota(jnp.int32, (NBLK, NBLK), 0)
    slot_v[...] = jnp.sum(jnp.where(held_blocks == wanted, number, 0), axis=0, keepdims=True)
    to_scalars = pltpu.make_async_copy(slot_v, slot_of, own_sem.at[8])
    to_scalars.start()

    def one_peer(f, d):
        return x_peer(d) if f == 0 else y_peer(d)

    firsts, seconds, siblings, wide = {}, {}, {}, {}

    def spread(i, f, d):
        dx, dy = (-d, 0) if f == 0 else (0, -d)
        here = bufs[i].at[:, (x + dx) % X, (y + dy) % Y, core, f]
        for e in (1, 3):
            seconds[i, f, d, e] = go(remote(
                here, here, two_send.at[i, f, d, e], two_recv.at[i, f, d, e], one_peer(1 - f, e)
            ))

    def relay(i, f, d):
        for a, e in ((0, 1), (1, 3)):
            seconds[i, f, d, e].wait_recv()
            dx, dy = (-d, -e) if f == 0 else (-e, -d)
            here = bufs[i].at[a, (x + dx) % X, (y + dy) % Y, core, f]
            seconds[i, f, d, 2 * a] = go(remote(
                here, here, two_send.at[i, f, d, 2 * a], two_recv.at[i, f, d, 2 * a],
                one_peer(1 - f, e),
            ))

    def to_sibling(i, f, e):
        for d in range(4):
            if e == 2:
                seconds[i, f, d, 0].wait_recv()
                seconds[i, f, d, 2].wait_recv()
        if f == 0:
            here = bufs[i].at[:, :, (y - e) % Y, core, f]
        else:
            here = bufs[i].at[:, (x - e) % X, :, core, f]
        siblings[i, f, e] = go(remote(
            here, here, core_send.at[i, f, e], core_recv.at[i, f, e], sibling
        ))

    def begin(i):
        for n in range(len(peers)):
            small[i, n].wait_recv()
        local[i].wait()
        for d in (2, 1, 3):
            for f in range(2):
                here = bufs[i].at[:, x, y, core, f]
                firsts[i, f, d] = go(remote(
                    here, here, one_send.at[i, f, d - 1], one_recv.at[i, f, d - 1], one_peer(f, d)
                ))
        for f in range(2):
            spread(i, f, 0)

    def go_on(i, d):
        for f in range(2):
            firsts[i, f, d].wait_recv()
            spread(i, f, d)

    begin(0)
    for i, (ref, to) in enumerate(((q, q_in), (g, g_in))):
        for d in (2, 1, 3):
            peer = (t + d) % TP
            wide[i, d] = go(remote(
                ref.at[:, columns(peer, WIDE)], to.at[rows_of(t, MINE), :],
                wide_send.at[i, d - 1], wide_recv.at[i, d - 1], (c, peer),
            ))
    begin(1)
    for i in range(2):
        for d in (1, 3, 2):
            go_on(i, d)
    for i in range(2):
        for d in (0, 1, 3, 2):
            for f in range(2):
                relay(i, f, d)
        for e in (0, 1, 3):
            for f in range(2):
                to_sibling(i, f, e)
    for f in range(2):
        to_sibling(0, f, 2)

    def by_head(i, ref, to):
        for d in (1, 2, 3):
            wide[i, d].wait_recv()
        local[2 + i].wait()
        for b in range(2):
            here = pl.ds(b * BLOCK, BLOCK)
            for h in range(GROUP):
                to[b, pl.ds(h * BLOCK, BLOCK), :] = ref[here, pl.ds(h * HEAD, HEAD)]

    by_head(0, q_in, qh)

    offset = lax.broadcasted_iota(jnp.int32, (1, LANES), 1) % BLOCK
    base, low = [], []
    for b in range(2):
        block = row_block[2 * c + b]
        position = block * BLOCK + offset
        lowest = jnp.zeros((1, LANES), jnp.int32)
        end = jnp.int32(0)
        for d in range(DOCS):
            end = end + doc[d]
            lowest = jnp.where(position >= end, end, lowest)
        base.append(block - BACK)
        low.append(lowest - (block - BACK) * BLOCK)

    def in_order(i, to):
        for f in range(2):
            for e in range(4):
                siblings[i, f, e].wait_recv()

        def window(j, carry):
            rows = pl.ds(pl.multiple_of(j * BLOCK, BLOCK), BLOCK)
            for b in range(2):
                s = slot_of[0, jnp.maximum(base[b] + j, 0)]
                at = tuple(
                    lax.rem(lax.div(s, n), m) for n, m in ((64, 2), (16, 4), (4, 4), (2, 2), (1, 2))
                )
                to[b, rows, :] = bufs[i][at]
            return carry

        lax.fori_loop(0, BACK + 1, window, 0, unroll=11)

    to_scalars.wait()
    in_order(0, kwin)

    def keys_of(tile):
        return pl.ds(pl.multiple_of(tile * TILE, TILE), TILE)

    tail = pl.ds(BACK * BLOCK, BLOCK)
    at_tile = lax.broadcasted_iota(jnp.int32, (TILE, LANES), 0)
    at_tail = lax.broadcasted_iota(jnp.int32, (BLOCK, LANES), 0)

    def folded(values, fold):
        return fold(values.reshape(values.shape[0] // 8, 8, LANES), axis=0)

    def scores(tile, tops):
        out = []
        for b in range(2):
            s = mm(kwin[b, keys_of(tile), :], qh[b], 1, 1)
            s = jnp.where(at_tile >= low[b] - tile * TILE, s, NEGATIVE)
            s_scr[b, keys_of(tile), :] = s
            out.append(jnp.maximum(tops[b], folded(s, jnp.max)))
        return tuple(out)

    tops = []
    for b in range(2):
        s = mm(kwin[b, tail, :], qh[b], 1, 1)
        seen = (at_tail >= low[b] - BACK * BLOCK) & (at_tail <= offset)
        s = jnp.where(seen, s, NEGATIVE)
        s_scr[b, tail, :] = s
        tops.append(folded(s, jnp.max))
    tops = lax.fori_loop(0, TILES, scores, tuple(tops), unroll=TILES)
    tops = [jnp.max(top, axis=0, keepdims=True) for top in tops]

    for f in range(2):
        to_sibling(1, f, 2)
    by_head(1, g_in, gh)
    in_order(1, vwin)

    def weigh_part(b, part, total, acc):
        w = jnp.exp2((s_scr[b, part, :] - tops[b]) * SCALE2)
        total = total + folded(w, jnp.sum)
        w16 = w.astype(bf16)
        w_scr[b, part, :] = w16
        return total, acc + mm(vwin[b, part, :], w16, 0, 0)

    def weigh(tile, state):
        out = [weigh_part(b, keys_of(tile), *state[b]) for b in range(2)]
        return tuple(out)

    state = tuple(
        weigh_part(b, tail, jnp.zeros((8, LANES), f32), jnp.zeros((HEAD, LANES), f32))
        for b in range(2)
    )
    state = lax.fori_loop(0, TILES, weigh, state, unroll=TILES)

    inverse, inv_rows, delta = [], [], []
    for b in range(2):
        inv = 1.0 / jnp.sum(state[b][0], axis=0, keepdims=True)
        inverse.append(inv)
        inv_rows.append(jnp.broadcast_to(inv, (HEAD, LANES)).T)
        gs[b] = (gh[b].astype(f32) * inv_rows[b]).astype(bf16)

    results = []

    def send_rows(i, ref, out):
        for d in (2, 1, 3):
            peer = (t + d) % TP
            results.append(go(remote(
                ref.at[rows_of(peer, MINE), :], out.at[:, columns(t, WIDE)],
                res_send.at[i, d - 1], res_recv.at[i, d - 1], (c, peer),
            )))
        local[4 + i] = pltpu.make_async_copy(
            ref.at[rows_of(t, MINE), :], out.at[:, columns(t, WIDE)], own_sem.at[4 + i]
        )
        local[4 + i].start()

    def value_part(b, part, first):
        dv = mm(w_scr[b, part, :], gs[b], 1, 0)
        dv_rel[b, pl.ds(first + 1, dv.shape[0] // BLOCK)] = dv.reshape(-1, BLOCK, HEAD)

    def value_tile(tile, carry):
        for b in range(2):
            value_part(b, keys_of(tile), tile * (TILE // BLOCK))
        return carry

    for b in range(2):
        value_part(b, tail, BACK)
    lax.fori_loop(0, TILES, value_tile, 0, unroll=TILES)

    rels = (dk_rel, dv_rel)
    for ref in rels:
        for b in range(2):
            for zero in (0, BACK + 2):
                ref[b, zero] = jnp.zeros((BLOCK, HEAD), f32)

    def piece(i, f, d, e, a, which):
        dx, dy = (d, e) if f == 0 else (e, d)
        s = ctx_of(a, (x + dx) % X, (y + dy) % Y, which) * 2 + f
        total = None
        for b in range(2):
            rel = row_block[s] - base[b] + 1
            part = rels[i][b, jnp.minimum(jnp.maximum(rel, 0), BACK + 2)]
            total = part if total is None else total + part
        return total

    order = [(d, f) for d in (2, 1, 3, 0) for f in range(2)]
    r0 = {}

    def assemble(i):
        for d, f in order:
            def fill(e, carry):
                for a in range(ZH):
                    out_core[i, f, d, e, a] = piece(i, f, d, e, a, 1 - core).astype(bf16)
                return carry

            lax.fori_loop(0, 4, fill, 0, unroll=4)
            r0[i, f, d] = go(remote(
                out_core.at[i, f, d], in_core.at[i, f, d],
                r0_send.at[i, f, d], r0_recv.at[i, f, d], sibling,
            ))

    def r1(i, f, d, e):
        return remote(
            held.at[i, f, d, e], in_one.at[i, f, d - 1, e], r1_send.at[i, f, d - 1, e],
            r1_recv.at[i, f, d - 1, e], one_peer(f, d),
        )

    def join(i):
        for d, f in order:
            r0[i, f, d].wait_recv()

            def add(n, carry):
                e = (n + 1) % 4
                for a in range(ZH):
                    total = piece(i, f, d, e, a, core) + in_core[i, f, d, e, a].astype(f32)
                    held[i, f, d, e, a] = total.astype(bf16)
                if d > 0:
                    r1(i, f, d, e).start()
                return carry

            lax.fori_loop(0, 4, add, 0, unroll=4)

    def back_part(b, part, first, dq_t):
        keys = kwin[b, part, :]
        dp = mm(vwin[b, part, :], gh[b], 1, 1)
        ds = (w_scr[b, part, :].astype(f32) * (dp - delta[b])).astype(bf16)
        dk = mm(ds, qs[b], 1, 0)
        dk_rel[b, pl.ds(first + 1, dk.shape[0] // BLOCK)] = dk.reshape(-1, BLOCK, HEAD)
        return dq_t + mm(keys, ds, 0, 0)

    def back(b):
        def step(tile, dq_t):
            return back_part(b, keys_of(tile), tile * (TILE // BLOCK), dq_t)

        dq_t = back_part(b, tail, BACK, jnp.zeros((HEAD, LANES), f32))
        dq_t = lax.fori_loop(0, TILES, step, dq_t, unroll=TILES)
        dq = (dq_t * (inverse[b] * SCALE)).T.astype(bf16)
        for h in range(GROUP):
            g_in[pl.ds(b * BLOCK, BLOCK), pl.ds(h * HEAD, HEAD)] = dq[h * BLOCK : (h + 1) * BLOCK]

    assemble(1)
    for b in range(2):
        att_t = state[b][1] * inverse[b]
        delta.append(jnp.sum(gh[b].astype(f32).T * att_t, axis=0, keepdims=True))
        att = att_t.T.astype(bf16)
        qs[b] = (qh[b].astype(f32) * (inv_rows[b] * SCALE)).astype(bf16)
        for h in range(GROUP):
            q_in[pl.ds(b * BLOCK, BLOCK), pl.ds(h * HEAD, HEAD)] = att[h * BLOCK : (h + 1) * BLOCK]
    send_rows(0, q_in, att_o)
    join(1)
    back(0)
    back(1)
    assemble(0)
    send_rows(1, g_in, dq_o)
    join(0)

    def r2(i, f, e):
        return remote(
            held_two.at[i, f, e], in_two.at[i, f, e - 1], r2_send.at[i, f, e - 1],
            r2_recv.at[i, f, e - 1], one_peer(1 - f, e),
        )

    for i in (1, 0):
        for e in (1, 2, 3, 0):
            for f in range(2):
                for d in (1, 3, 2):
                    r1(i, f, d, e).wait_recv()
                for a in range(ZH):
                    total = held[i, f, 0, e, a].astype(f32)
                    for d in range(3):
                        total = total + in_one[i, f, d, e, a].astype(f32)
                    held_two[i, f, e, a] = total.astype(bf16)
                if e > 0:
                    go(r2(i, f, e))

    last = {}
    for i in (1, 0):
        for f in range(2):
            for e in (1, 2, 3):
                r2(i, f, e).wait_recv()
            for a in range(ZH):
                total = held_two[i, f, 0, a].astype(f32)
                for e in range(3):
                    total = total + in_two[i, f, e, a].astype(f32)
                held_z[i, a, f] = total.astype(bf16)
        for n, peer in enumerate(peers):
            a = (zh + (n + 1) // TP) % ZH
            last[i, n] = go(remote(
                held_z.at[i, a, peer[1] // 2, pl.ds(pl.multiple_of((peer[1] % 2) * MINE, MINE), MINE), :],
                fins[i].at[zh, t], r3_send.at[i, n], r3_recv.at[i, n], peer,
            ))
        local[6 + i] = pltpu.make_async_copy(
            held_z.at[i, zh, t // 2, mine, :], fins[i].at[zh, t], own_sem.at[6 + i]
        )
        local[6 + i].start()
    for copy in last.values():
        copy.wait_recv()
    for copy in results:
        copy.wait_recv()
    for i in range(4, 8):
        local[i].wait()
    for copy in sends:
        copy.wait_send()
    for i in range(2):
        for f in range(2):
            for d in range(1, 4):
                for e in range(4):
                    r1(i, f, d, e).wait_send()


def fused(doc_lengths, row_block, queries, keys, values, out_grad):
    dma = pltpu.SemaphoreType.DMA
    anywhere = pl.BlockSpec(memory_space=pl.ANY)
    smem = pl.BlockSpec(memory_space=pltpu.SMEM)
    V = pltpu.VMEM
    slots = (ZH, X, Y, CORE, 2, BLOCK, HEAD)
    piece = (BLOCK, HEAD)
    return pl.pallas_call(
        fused_kernel,
        out_shape=(
            jax.ShapeDtypeStruct((MINE, TP * WIDE), bf16),
            jax.ShapeDtypeStruct((MINE, TP * WIDE), bf16),
            jax.ShapeDtypeStruct((ZH, TP, MINE, HEAD), bf16),
            jax.ShapeDtypeStruct((ZH, TP, MINE, HEAD), bf16),
        ),
        in_specs=[smem, smem, pl.BlockSpec(memory_space=pltpu.VMEM)] + [anywhere] * 4,
        out_specs=[anywhere] * 4,
        scratch_shapes=[
            V(slots, bf16), V(slots, bf16),
            V((ROWS, WIDE), bf16), V((ROWS, WIDE), bf16),
            V((2, WINDOW, HEAD), bf16), V((2, WINDOW, HEAD), bf16),
            V((2, LANES, HEAD), bf16), V((2, LANES, HEAD), bf16),
            V((2, LANES, HEAD), bf16), V((2, LANES, HEAD), bf16),
            V((2, WINDOW, LANES), f32), V((2, WINDOW, LANES), bf16),
            V((2, BACK + 3, BLOCK, HEAD), f32), V((2, BACK + 3, BLOCK, HEAD), f32),
            V((1, NBLK), jnp.int32), pltpu.SMEM((1, NBLK), jnp.int32),
            V((2, 2, 4, 4, ZH) + piece, bf16), V((2, 2, 4, 4, ZH) + piece, bf16),
            V((2, 2, 4, 4, ZH) + piece, bf16), V((2, 2, 3, 4, ZH) + piece, bf16),
            V((2, 2, 4, ZH) + piece, bf16), V((2, 2, 3, ZH) + piece, bf16),
            V((2, ZH, 2) + piece, bf16),
            dma((9,)),
            dma((2, 7)), dma((2, 7)),
            dma((2, 3)), dma((2, 3)),
            dma((2, 2, 3)), dma((2, 2, 3)),
            dma((2, 2, 4, 4)), dma((2, 2, 4, 4)),
            dma((2, 2, 4)), dma((2, 2, 4)),
            dma((2, 3)), dma((2, 3)),
            dma((2, 2, 4)), dma((2, 2, 4)),
            dma((2, 2, 3, 4)), dma((2, 2, 3, 4)),
            dma((2, 2, 3)), dma((2, 2, 3)),
            dma((2, 7)), dma((2, 7)),
        ],
        compiler_params=pltpu.CompilerParams(
            collective_id=0, has_side_effects=True, vmem_limit_bytes=VMEM_LIMIT
        ),
        name="fused",
    )(doc_lengths, row_block, row_block.reshape(1, NBLK), queries, keys, values, out_grad)


def hand_over_kernel(*refs):
    held, sums, sems = refs[8:12], refs[12:14], refs[14]
    arrive = [pltpu.make_async_copy(refs[i], held[i], sems.at[0, i]) for i in range(4)]
    from_where = held[:2] + sums
    leave = [pltpu.make_async_copy(from_where[i], refs[4 + i], sems.at[1, i]) for i in range(4)]
    for copy in arrive:
        copy.start()
    for i in range(4):
        arrive[i].wait()
        if i >= 2:
            for h in range(TP):
                total = held[i][0, h].astype(f32) + held[i][1, h].astype(f32)
                sums[i - 2][:, pl.ds(h * HEAD, HEAD)] = total.astype(bf16)
        leave[i].start()
    for copy in leave:
        copy.wait()


def hand_over(arrays):
    anywhere = pl.BlockSpec(memory_space=pl.ANY)
    narrow = jax.ShapeDtypeStruct((MINE, TP * HEAD), bf16)
    return pl.pallas_call(
        hand_over_kernel,
        out_shape=tuple(jax.ShapeDtypeStruct(a.shape, a.dtype) for a in arrays[:2]) + (narrow,) * 2,
        in_specs=[anywhere] * 4,
        out_specs=[anywhere] * 4,
        scratch_shapes=[pltpu.VMEM(a.shape, a.dtype) for a in arrays]
        + [pltpu.VMEM(narrow.shape, bf16)] * 2
        + [pltpu.SemaphoreType.DMA((2, 4))],
        name="hand_over",
    )(*arrays)


def per_device(queries, keys, values, out_grad, doc_lengths, row_block):
    return hand_over(fused(doc_lengths, row_block, queries, keys, values, out_grad))


def solution(mesh):
    return jax.shard_map(
        per_device,
        mesh=mesh,
        in_specs=(P(("ctx", "tp"), None),) * 4 + (P(), P()),
        out_specs=(P(("ctx", "tp"), None),) * 4,
        check_vma=False,
    )
```
